256 devices in a mesh: vir: 64 (over x, z, core), trip: 4 (over y).
Axes of the slice: x: 4, y: 4, z: 8, core: 2. Of those that a mesh axis runs over, the one named last changes fastest.
Arguments:
- triplets: int32 [4, 3], P('trip'), may hold values from 0 to 119, as said below
- pair_integrals: bfloat16 [2, 448, 448, 448], P(None, 'vir'), may hold values from -16 to 16
- k_integrals: bfloat16 [4, 448, 448, 448], P('trip', 'vir'), may hold values from -16 to 16
- pair_amplitudes: bfloat16 [448, 448], replicated, may hold values from -0.25 to 0.25
- k_amplitudes: bfloat16 [4, 2, 448, 448], P('trip'), may hold values from -0.25 to 0.25
- occ_energy: float32 [120], replicated, may hold values from -3 to -0.2
- vir_energy: float32 [448], replicated, may hold values from 0.1 to 1.5
Outputs:
- energies: float32 [4], P('trip')
- vv_density: float32 [448, 448], P('vir')
- vvvo_density: bfloat16 [4, 448, 448, 448], P('trip', 'vir')
The draws below stay inside these ranges and needn't reach their ends.
Inputs may be any that keep to these rules, and one draw needn't show every extreme that they name: `triplets`: in every row the first two numbers are the same two different occupied orbitals; the third numbers differ from each other and from those two.
All inputs are finite; a program needn't handle non-finite values.
Results may differ from the reference program's by a relative error of at most 0.0052.
Values may be sent and summed in bfloat16 or wider, within the bound.
A program may use at most 128 MiB of HBM per device.

```python
import jax
import jax.numpy as jnp
from jax import lax

V = 448
O = 120
TRIPS = 4


def draw_triplets(key, part):
    key = jax.random.fold_in(key, 11)
    order = jax.random.permutation(key, O)
    picked = order[:2 + TRIPS].astype(jnp.int32)
    slot = jax.random.randint(jax.random.fold_in(key, 1), (), 0, 2 + TRIPS)
    placed = picked.at[slot].set(O - 1)
    picked = jnp.where(jnp.max(picked) == O - 1, picked, placed)
    first = jnp.full((TRIPS,), picked[0], jnp.int32)
    second = jnp.full((TRIPS,), picked[1], jnp.int32)
    return jnp.stack([first, second, picked[2:]], axis=1).astype(jnp.int32)


def raised(entries, key, source, target, parts, factor):
    def block_of(dim):
        return (jnp.arange(entries.shape[dim]) // (entries.shape[dim] // parts)).reshape((-1,) + (1,) * (entries.ndim - 1 - dim))

    first = jax.random.permutation(key, parts)[block_of(target)]
    far = (block_of(target) + parts // 2) % parts
    return jnp.where((block_of(source) == first) | (block_of(source) == far), factor * entries, entries)


def steps_of(stream_key, shape, split, low, top_value):
    loudness, own = 1.0, jax.random.fold_in(stream_key, 6)
    for position, blocks in split:
        steps = jnp.exp(jax.random.uniform(jax.random.fold_in(own, position), (blocks,), jnp.float32, low / len(split), top_value / len(split)))
        loudness = loudness * jnp.repeat(steps, shape[position] // blocks).reshape([-1 if axis == position else 1 for axis in range(len(shape))])
    return loudness


def scatter_about(key, shape, spread, reach, cuts=(), dtype=jnp.bfloat16):
    drawn = spread * jax.random.normal(key, shape, jnp.float32)
    if cuts:
        drawn = drawn * steps_of(key, shape, cuts, -0.22, 0.18)
    return jnp.clip(drawn, -reach, reach).astype(dtype)


def gaussian_with(rng, extent, scale, most, shards, heavy, held_as=jnp.bfloat16):
    array = scale * jax.random.normal(rng, extent, jnp.float32)
    if shards:
        array = array * steps_of(rng, extent, shards, -0.22, 0.18)
    return jnp.clip(raised(array, jax.random.fold_in(rng, 3), *heavy), -most, most).astype(held_as)


def setup_inputs(seed: int = 0) -> dict:
    key_list = jax.random.split(jax.random.key(seed), 8)
    triplets = draw_triplets(jax.random.fold_in(key_list[7], 71), 0)
    pair_integrals = gaussian_with(key_list[1], (2, V, V, V), 1.0, 16.0, ((1, 64),), (1, 2, 64, 4.0))
    k_integrals = gaussian_with(key_list[2], (TRIPS, V, V, V), 1.0, 16.0, ((0, 4), (1, 64)), (1, 2, 64, 4.0))
    pair_amplitudes = scatter_about(key_list[3], (V, V), V ** -0.5, 0.25)
    k_amplitudes = scatter_about(key_list[4], (TRIPS, 2, V, V), V ** -0.5, 0.25, ((0, 4),))
    occ_energy = jnp.clip(jax.random.uniform(key_list[5], (O,), jnp.float32, -3.0, -0.2), -3.0, -0.2)
    vir_energy = jnp.clip(jax.random.uniform(key_list[6], (V,), jnp.float32, 0.1, 1.5), 0.1, 1.5)
    return dict(triplets=triplets, pair_integrals=pair_integrals, k_integrals=k_integrals, pair_amplitudes=pair_amplitudes, k_amplitudes=k_amplitudes, occ_energy=occ_energy, vir_energy=vir_energy)


def rounded(value):
    return lax.optimization_barrier(value.astype(jnp.bfloat16)).astype(jnp.float32)


def reference(triplets, pair_integrals, k_integrals, pair_amplitudes, k_amplitudes, occ_energy, vir_energy):
    slab_i = pair_integrals[0].astype(jnp.float32)
    slab_j = pair_integrals[1].astype(jnp.float32)
    t_ij = pair_amplitudes.astype(jnp.float32)

    def one_triplet(inputs):
        row, slab_k, amps = inputs
        slab_k = slab_k.astype(jnp.float32)
        t_ik = amps[0].astype(jnp.float32)
        t_jk = amps[1].astype(jnp.float32)
        shift = occ_energy[row[0]] + occ_energy[row[1]] + occ_energy[row[2]]
        own = jnp.einsum('acd,bd->abc', slab_i, t_jk) + jnp.einsum('abd,dc->abc', slab_i, t_jk)
        b_terms = rounded(jnp.einsum('bcd,ad->abc', slab_j, t_ik) + jnp.einsum('bad,dc->abc', slab_j, t_ik))
        c_terms = rounded(jnp.einsum('cbd,ad->abc', slab_k, t_ij) + jnp.einsum('cad,db->abc', slab_k, t_ij))
        amplitude = own + b_terms + c_terms
        denominator = vir_energy[:, None, None] + vir_energy[None, :, None] + vir_energy[None, None, :] - shift
        energy = jnp.sum(amplitude * amplitude / denominator) / (V ** 3)
        weighted = (amplitude / denominator).astype(jnp.bfloat16)
        flat = weighted.reshape(V * V, V)
        gram = jnp.dot(flat.T, flat, preferred_element_type=jnp.float32)
        wide = weighted.astype(jnp.float32)
        gamma = jnp.einsum('ayc,ad->cyd', wide, t_ij) + jnp.einsum('ybc,db->cyd', wide, t_ij)
        return energy, gram, gamma.astype(jnp.bfloat16)

    energies, grams, gammas = lax.map(one_triplet, (triplets, k_integrals, k_amplitudes))
    density = jnp.sum(grams, axis=0) / (V * V)
    return energies, density, gammas
```

```python
import numpy as np
import jax
import jax.numpy as jnp
from jax import lax
from jax.experimental import pallas as pl
from jax.experimental.pallas import tpu as pltpu
from jax.sharding import PartitionSpec as P

MESH = pl.DeviceIdType.MESH
BF, F32 = jnp.bfloat16, jnp.float32
V = 448
N = 64
L = 7
GROUPS = 4
GD = 16
GR = GD * L
SLOT = 64
ROWS_A, ROWS_B = 112, 80
QUARTER = 48


def pack_matrix():
    m = np.zeros((GD, SLOT, L, GD, L), np.float32)
    for p in range(L):
        for q in range(L):
            for j in range(GD):
                m[j, L * p + q, p, j, q] = 1
    m[:, 49] = m[:, 48]
    return m.reshape(GD * SLOT, L * GR)


def unpack_matrix():
    m = np.zeros((L, GD, L, GD, SLOT), np.float32)
    for p in range(L):
        for q in range(L):
            for k in range(GD):
                m[q, k, p, k, L * p + q] = 1
    return m.reshape(L * GR, GD * SLOT)


def row_matrix():
    m = np.zeros((N, 8, N, L), np.float32)
    for j in range(N):
        for i in range(L):
            m[j, i, j, i] = 1
    return m.reshape(N * 8, V)


def nn(x, y):
    return lax.dot_general(x, y, (((1,), (0,)), ((), ())), preferred_element_type=F32)


def nt(x, y):
    return lax.dot_general(x, y, (((1,), (1,)), ((), ())), preferred_element_type=F32)


def tn(x, y):
    return lax.dot_general(x, y, (((0,), (0,)), ((), ())), preferred_element_type=F32)


def iota(shape, dim):
    return lax.broadcasted_iota(jnp.int32, shape, dim)


def packed_a(x, pk):
    o = nn(pk[...], x).reshape(GD, SLOT, 256)
    last = jnp.where(iota((GD, 16, 128), 1) == 0, o[:, 48:64, :128], o[:, 48:64, 128:])
    return o[:, :48, :128].astype(BF), o[:, :48, 128:].astype(BF), last.astype(BF)


def packed_b(x, pk):
    o = nn(pk[...], x).reshape(GD, SLOT, 256)
    row = iota((GD, 32, 128), 1)
    full = jnp.broadcast_to(o[:, 48:49, :128], (GD, 32, 128))
    half = o[:, 32:64, 128:]
    high = jnp.where(row == 30, full, half)
    high = jnp.where(row == 31, full, pltpu.roll(high, 64, 2))
    mixed = jnp.where(iota((GD, 32, 128), 2) < 64, o[:, :32, 128:], high)
    return o[:, :48, :128].astype(BF), mixed.astype(BF)


def spread_a(m0, m1, last, tmp):
    last = last.astype(F32)
    second = jnp.broadcast_to(last[:, 1:2, :], (GD, 16, 128)).astype(BF)
    last = last.astype(BF)
    left = jnp.concatenate([m0, last], axis=1).reshape(GD * SLOT, 128)
    right = jnp.concatenate([m1, second], axis=1).reshape(GD * SLOT, 128)
    tmp[:, 0:128] = left
    tmp[:, 128:256] = right


def spread_b(m0, mixed, tmp):
    mixed = mixed.astype(F32)
    lane = iota((GD, 32, 128), 2) < 64
    turned = pltpu.roll(mixed, 64, 2)
    low = jnp.where(lane, mixed, 0.0).astype(BF)
    high = jnp.where(lane, turned, 0.0).astype(BF)
    row = jnp.where(
        iota((GD, 1, 128), 2) < 64, turned[:, 30:31, :], mixed[:, 31:32, :]
    )
    full = jnp.broadcast_to(row, (GD, 16, 128)).astype(BF)
    left = jnp.concatenate([m0, full], axis=1).reshape(GD * SLOT, 128)
    right = jnp.concatenate([low, high], axis=1).reshape(GD * SLOT, 128)
    tmp[:, 0:128] = left
    tmp[:, 128:256] = right


def kernel(
    trip_ref, occ_ref, virs_ref, vir_ref, pair_hbm, k_hbm, tij, kamp, pk, up, rowm,
    energy_ref, density_ref, vvvo_hbm,
    gi, gj, gk, cs, w, xb, tjt, tit, vrow, tmp,
    g_send, g_recv, sa_send, sa_recv, sb_send, sb_recv, ya_send, ya_recv, yb_send, yb_recv,
    gram, d1, d2, d2s, dfin, out_a,
    ld, g_ss, g_zs, y_ss, y_l, y_r, y_o, a_ss, a_rs, d1_ss, d1_rs, d2_ss, d2_rs, d3_ss, d3_rs,
):
    v = lax.axis_index("vir")
    y = lax.axis_index("trip")
    core = lax.rem(v, 2)
    grp = v // GD
    inner = lax.rem(v, GD)
    chip = v // 2

    load_j = pltpu.make_async_copy(pair_hbm.at[1], gj, ld.at[0])
    load_k = pltpu.make_async_copy(k_hbm.at[0], gk, ld.at[1])
    load_i = pltpu.make_async_copy(pair_hbm.at[0], gi, ld.at[2])
    load_j.start()
    load_k.start()
    load_i.start()

    barrier = pltpu.get_barrier_semaphore()

    def greet(k, c):
        pl.semaphore_signal(
            barrier, inc=1, device_id={"vir": lax.rem(v + k, N), "trip": y}, device_id_type=MESH
        )
        return c

    lax.fori_loop(1, N, greet, 0)
    partner = chip * 2 + (1 - core)
    for dy in (1, 2, 3):
        ty = lax.rem(y + dy, 4)
        pl.semaphore_signal(barrier, inc=1, device_id={"vir": v, "trip": ty}, device_id_type=MESH)
        pl.semaphore_signal(
            barrier, inc=1, device_id={"vir": partner, "trip": ty}, device_id_type=MESH
        )

    tjt[...] = kamp[0, 1].astype(F32).T.astype(BF)
    tit[...] = kamp[0, 0].astype(F32).T.astype(BF)
    vrow[...] = jnp.ones_like(vrow)
    vrow[0:1, 0:V] = vir_ref[...]

    load_j.wait()
    xb[:, :, 384:512] = jnp.zeros((L, V, 128), BF)
    xb[:, :, 0:V] = gj[...]

    def send_group(src, dst, g, ss, rs):
        def one(k, c):
            d = g * GD + lax.rem(inner + k, GD)

            @pl.when(d != v)
            def _():
                pltpu.make_async_remote_copy(
                    src_ref=src.at[d], dst_ref=dst.at[v], send_sem=ss, recv_sem=rs,
                    device_id={"vir": d, "trip": y}, device_id_type=MESH,
                ).start()

            @pl.when(d == v)
            def _():
                pltpu.make_async_copy(src.at[d], dst.at[v], rs).start()

            return c

        lax.fori_loop(0, GD, one, 0)

    def rows_of(g):
        return pl.ds(pl.multiple_of(g * GR, 16), GR)

    def slots_of(g):
        return pl.ds(g * GD, GD)

    def turn(s, c):
        g = lax.rem(grp + s, GROUPS)
        m0, m1, last = packed_a(xb[:, rows_of(g), 0:256].reshape(L * GR, 256), pk)
        g_send[0, slots_of(g)] = m0
        g_send[1, slots_of(g)] = m1
        g_send[2, slots_of(g), 0:16] = last
        m0, mixed = packed_b(xb[:, rows_of(g), 256:512].reshape(L * GR, 256), pk)
        g_send[3, slots_of(g)] = m0
        g_send[2, slots_of(g), 16:48] = mixed

        @pl.when(s == 0)
        def _():
            pl.semaphore_wait(barrier, N - 1 + 6)

        send_group(g_send.at[y], g_recv.at[y], g, g_ss, g_zs.at[grp])
        return c

    lax.fori_loop(0, GROUPS, turn, 0)

    t_ij = tij[...]
    load_k.wait()

    def c_part(c, carry):
        x = gk[c]
        cs[c] = nt(t_ij, x) + nn(x, t_ij)
        return carry

    lax.fori_loop(0, L, c_part, 0)

    up_y, down_y = lax.rem(y + 1, 4), lax.rem(y + 3, 4)

    def y_copy(q, g, ty, rs):
        return pltpu.make_async_remote_copy(
            src_ref=g_recv.at[q, slots_of(g)], dst_ref=g_recv.at[q, slots_of(g)],
            send_sem=y_ss, recv_sem=rs, device_id={"vir": v, "trip": ty}, device_id_type=MESH,
        )

    for s in range(GROUPS):
        g = s
        y_copy(y, g, up_y, g_zs.at[g]).wait_recv()
        y_copy(y, g, up_y, y_l.at[g]).start()
        y_copy(y, g, down_y, y_r.at[g]).start()

    load_i.wait()
    w[:, :, 384:512] = jnp.zeros((L, V, 128), F32)

    def a_part(i, carry):
        x = gi[i]
        w[i, :, 0:V] = nt(x, kamp[0, 1]) + nt(tjt[...], x)
        return carry

    lax.fori_loop(0, L, a_part, 0)

    for g in range(GROUPS):
        y_copy(down_y, g, up_y, y_l.at[g]).wait_recv()
        if g < 2:
            y_copy(down_y, g, up_y, y_o.at[g]).start()
        y_copy(up_y, g, up_y, y_r.at[g]).wait_recv()
        if g >= 2:
            y_copy(up_y, g, down_y, y_o.at[g]).start()
    for g in range(GROUPS):
        y_copy(lax.rem(y + 2, 4), g, up_y, y_o.at[g]).wait_recv()

    def turned(g, c):
        spread_a(
            g_recv[0, slots_of(g)], g_recv[1, slots_of(g)], g_recv[2, slots_of(g), 0:16], tmp
        )
        o = nn(up[...], tmp[...])
        gj[:, rows_of(g), 0:256] = o.reshape(L, GR, 256).astype(BF)
        spread_b(g_recv[3, slots_of(g)], g_recv[2, slots_of(g), 16:48], tmp)
        o = nn(up[...], tmp[...])
        gj[:, rows_of(g), 256:V] = o.reshape(L, GR, 256)[:, :, 0:192].astype(BF)
        return c

    lax.fori_loop(0, GROUPS, turned, 0)

    def send_a(src, dst, n):
        def step(s, c):
            g = lax.rem(grp + s, GROUPS)
            m0, m1, last = packed_a(xb[:, rows_of(g), 0:256].reshape(L * GR, 256), pk)
            src[slots_of(g), 0:48] = m0
            src[slots_of(g), 48:96] = m1
            src[slots_of(g), 96:112] = last
            send_group(src, dst, g, a_ss.at[n], a_rs.at[n])
            return c

        lax.fori_loop(0, GROUPS, step, 0)

    def send_b(src, dst, n):
        def step(s, c):
            g = lax.rem(grp + s, GROUPS)
            m0, mixed = packed_b(xb[:, rows_of(g), 256:512].reshape(L * GR, 256), pk)
            src[slots_of(g), 0:48] = m0
            src[slots_of(g), 48:80] = mixed
            send_group(src, dst, g, a_ss.at[n], a_rs.at[n])
            return c

        lax.fori_loop(0, GROUPS, step, 0)

    def all_of(src, dst, n):
        return pltpu.make_async_remote_copy(
            src_ref=src, dst_ref=dst, send_sem=a_ss.at[n], recv_sem=a_rs.at[n],
            device_id={"vir": lax.rem(v + 1, N), "trip": y}, device_id_type=MESH,
        )

    def s_a(c, carry):
        xb[c, :, 0:256] = (cs[c, :, 0:256] + nt(kamp[0, 0], gj[c, 0:256])).astype(BF)
        return carry

    lax.fori_loop(0, L, s_a, 0)
    send_a(sa_send, sa_recv, 0)

    def s_b(c, carry):
        xb[c, :, 256:V] = (cs[c, :, 256:V] + nt(kamp[0, 0], gj[c, 256:V])).astype(BF)
        return carry

    lax.fori_loop(0, L, s_b, 0)
    send_b(sb_send, sb_recv, 1)

    def b_part(i, carry):
        w[i, :, 0:V] = w[i, :, 0:V] + nt(tit[...], gj[i])
        return carry

    lax.fori_loop(0, L, b_part, 0)

    shift = occ_ref[trip_ref[0, 0]] + occ_ref[trip_ref[0, 1]] + occ_ref[trip_ref[0, 2]]
    vcol = jnp.sum(
        jnp.where(iota((V, V), 0) == iota((V, V), 1), vrow[0:1, 0:V], 0.0), axis=1, keepdims=True
    )

    def weigh(lanes, e):
        def one(i, e):
            x = w[i, :, lanes]
            den = vcol + (vrow[0:1, lanes] + (virs_ref[v * L + i] - shift))
            z = x / den
            xb[i, :, lanes] = z.astype(BF)
            return e + jnp.sum(x * z, axis=0, keepdims=True)

        return lax.fori_loop(0, L, one, e)

    all_of(sa_send, sa_recv, 0).wait_recv()

    def add_a(g, c):
        spread_a(
            sa_recv[slots_of(g), 0:48], sa_recv[slots_of(g), 48:96], sa_recv[slots_of(g), 96:112],
            tmp,
        )
        o = nn(up[...], tmp[...]).reshape(L, GR, 256)
        w[:, rows_of(g), 0:256] = w[:, rows_of(g), 0:256] + o
        return c

    lax.fori_loop(0, GROUPS, add_a, 0)
    e = weigh(slice(0, 256), jnp.zeros((1, 256), F32))
    send_a(ya_send, ya_recv, 2)

    def gram_a(i, acc):
        x = xb[i, :, 0:256]
        return acc + nt(x, x)

    cs[0] = lax.fori_loop(0, L, gram_a, jnp.zeros((V, V), F32))

    all_of(sb_send, sb_recv, 1).wait_recv()

    def add_b(g, c):
        spread_b(sb_recv[slots_of(g), 0:48], sb_recv[slots_of(g), 48:80], tmp)
        o = nn(up[...], tmp[...]).reshape(L, GR, 256)
        w[:, rows_of(g), 256:512] = w[:, rows_of(g), 256:512] + o
        return c

    lax.fori_loop(0, GROUPS, add_b, 0)
    e = weigh(slice(256, 512), e)
    send_b(yb_send, yb_recv, 3)

    def gram_b(i, acc):
        x = xb[i, :, 256:512]
        return acc + nt(x, x)

    total = lax.fori_loop(0, L, gram_b, cs[0])

    hi = total.astype(BF)
    rest = total - hi.astype(F32)
    mid = rest.astype(BF)
    lo = (rest - mid.astype(F32)).astype(BF)
    rows = nn(rowm[...], hi) + nn(rowm[...], mid) + nn(rowm[...], lo)
    energy = jnp.sum(e)
    gram[:, 384:512] = jnp.zeros((N * 8, 128), F32)
    gram[:, 0:V] = rows
    spare = lax.rem(iota((N * 8, 128), 0), 8) == 7
    mine = spare & (iota((N * 8, 128), 1) == y)
    gram[:, 0:128] = jnp.where(mine, energy, gram[:, 0:128])

    piece = y * 2 + core

    def piece_copy(k):
        to = lax.rem(piece + k, 8)
        return pltpu.make_async_remote_copy(
            src_ref=gram.at[pl.ds(pl.multiple_of(to * 64, 64), 64)], dst_ref=d1.at[piece],
            send_sem=d1_ss, recv_sem=d1_rs,
            device_id={"vir": chip * 2 + lax.rem(to, 2), "trip": to // 2}, device_id_type=MESH,
        )

    for k in range(1, 8):
        piece_copy(k).start()
    pltpu.make_async_copy(
        gram.at[pl.ds(pl.multiple_of(piece * 64, 64), 64)], d1.at[piece], d1_rs
    ).start()

    all_of(ya_send, ya_recv, 2).wait_recv()

    def take_a(g, c):
        spread_a(
            ya_recv[slots_of(g), 0:48], ya_recv[slots_of(g), 48:96], ya_recv[slots_of(g), 96:112],
            tmp,
        )
        o = nn(up[...], tmp[...]).reshape(L, GR, 256)
        gk[:, rows_of(g), 0:256] = o.astype(BF)
        return c

    lax.fori_loop(0, GROUPS, take_a, 0)

    def out_first(c, carry):
        x = gk[c, :, 0:256]
        cs[c] = nt(x, tij[:, 0:256])
        cs[c, 0:256] = cs[c, 0:256] + tn(x, tij[...])
        return carry

    lax.fori_loop(0, L, out_first, 0)

    pltpu.make_async_copy(d1, d1, d1_rs).wait()
    d2s[...] = jnp.sum(d1[...], axis=0)

    def owner_send(o, c):
        to = piece * 8 + o
        src = d2s.at[pl.ds(pl.multiple_of(o * 8, 8), 8)]

        @pl.when(to != v)
        def _():
            pltpu.make_async_remote_copy(
                src_ref=src, dst_ref=d2.at[chip], send_sem=d2_ss, recv_sem=d2_rs,
                device_id={"vir": to, "trip": y}, device_id_type=MESH,
            ).start()

        @pl.when(to == v)
        def _():
            pltpu.make_async_copy(src, d2.at[chip], d2_rs).start()

        return c

    lax.fori_loop(0, 8, owner_send, 0)

    is_owner = y == grp

    def fin_copy(ty):
        return pltpu.make_async_remote_copy(
            src_ref=dfin, dst_ref=dfin, send_sem=d3_ss, recv_sem=d3_rs,
            device_id={"vir": v, "trip": ty}, device_id_type=MESH,
        )

    @pl.when(is_owner)
    def _():
        pltpu.make_async_copy(d2, d2, d2_rs).wait()
        dfin[...] = jnp.sum(d2[...], axis=0)
        for dy in (1, 2, 3):
            fin_copy(lax.rem(y + dy, 4)).start()

    all_of(yb_send, yb_recv, 3).wait_recv()

    def take_b(g, c):
        spread_b(yb_recv[slots_of(g), 0:48], yb_recv[slots_of(g), 48:80], tmp)
        o = nn(up[...], tmp[...]).reshape(L, GR, 256)
        gk[:, rows_of(g), 256:V] = o[:, :, 0:192].astype(BF)
        return c

    lax.fori_loop(0, GROUPS, take_b, 0)

    def out_last(c, carry):
        x = gk[c, :, 256:V]
        acc = cs[c] + nt(x, tij[:, 256:V])
        gi[c, 0:256] = acc[0:256].astype(BF)
        gi[c, 256:V] = (acc[256:V] + tn(x, tij[...])).astype(BF)
        pltpu.make_async_copy(gi.at[c], vvvo_hbm.at[0, c], ld.at[0]).start()
        return carry

    lax.fori_loop(0, L, out_last, 0)

    @pl.when(jnp.logical_not(is_owner))
    def _():
        fin_copy(y).wait_recv()

    density_ref[...] = dfin[0:7, 0:V] * (1.0 / (V * V))
    sel = iota((1, 128), 1) == y
    es = jnp.sum(jnp.where(sel, dfin[7:8, 0:128], 0.0), axis=1, keepdims=True)
    energy_ref[...] = jnp.broadcast_to(es * (1.0 / V**3), (8, 128))

    pltpu.make_async_copy(gi, vvvo_hbm.at[0], ld.at[0]).wait()
    pltpu.make_async_remote_copy(
        src_ref=g_recv.at[y, pl.ds(0, N - 1)], dst_ref=g_recv.at[y, pl.ds(0, N - 1)],
        send_sem=g_ss, recv_sem=g_ss, device_id={"vir": v, "trip": up_y}, device_id_type=MESH,
    ).wait_send()
    pltpu.make_async_remote_copy(
        src_ref=g_recv.at[pl.ds(0, 3)], dst_ref=g_recv.at[pl.ds(0, 3)],
        send_sem=y_ss, recv_sem=y_ss, device_id={"vir": v, "trip": up_y}, device_id_type=MESH,
    ).wait_send()
    for n, buf in enumerate((sa_send, sb_send, ya_send, yb_send)):
        part = buf.at[pl.ds(0, N - 1)]
        all_of(part, part, n).wait_send()
    part = d1.at[pl.ds(0, 7)]
    pltpu.make_async_remote_copy(
        src_ref=part, dst_ref=part, send_sem=d1_ss, recv_sem=d1_ss,
        device_id={"vir": v, "trip": up_y}, device_id_type=MESH,
    ).wait_send()

    def drain_owner(count):
        q = d2.at[pl.ds(0, count)]
        pltpu.make_async_remote_copy(
            src_ref=q, dst_ref=q, send_sem=d2_ss, recv_sem=d2_ss,
            device_id={"vir": v, "trip": up_y}, device_id_type=MESH,
        ).wait_send()

    own_piece = (v // 8) == piece

    @pl.when(own_piece)
    def _():
        drain_owner(7)

    @pl.when(jnp.logical_not(own_piece))
    def _():
        drain_owner(8)

    @pl.when(is_owner)
    def _():
        for dy in (1, 2, 3):
            fin_copy(lax.rem(y + dy, 4)).wait_send()


def body(triplets, pair_integrals, k_integrals, pair_amplitudes, k_amplitudes, occ_energy, vir_energy):
    vm = pl.BlockSpec(memory_space=pltpu.VMEM)
    sm = pl.BlockSpec(memory_space=pltpu.SMEM)
    hbm = pl.BlockSpec(memory_space=pl.ANY)
    slab = pltpu.VMEM((L, V, V), BF)
    dma = pltpu.SemaphoreType.DMA
    energy, density, vvvo = pl.pallas_call(
        kernel,
        out_shape=(
            jax.ShapeDtypeStruct((8, 128), F32),
            jax.ShapeDtypeStruct((L, V), F32),
            jax.ShapeDtypeStruct((1, L, V, V), BF),
        ),
        in_specs=[sm, sm, sm, vm, hbm, hbm, vm, vm, vm, vm, vm],
        out_specs=(vm, vm, hbm),
        scratch_shapes=[
            slab, slab, slab,
            pltpu.VMEM((L, V, V), F32),
            pltpu.VMEM((L, V, 512), F32),
            pltpu.VMEM((L, V, 512), BF),
            pltpu.VMEM((V, V), BF),
            pltpu.VMEM((V, V), BF),
            pltpu.VMEM((8, 512), F32),
            pltpu.VMEM((GD * SLOT, 256), BF),
            pltpu.VMEM((4, N, QUARTER, 128), BF),
            pltpu.VMEM((4, N, QUARTER, 128), BF),
            pltpu.VMEM((N, ROWS_A, 128), BF),
            pltpu.VMEM((N, ROWS_A, 128), BF),
            pltpu.VMEM((N, ROWS_B, 128), BF),
            pltpu.VMEM((N, ROWS_B, 128), BF),
            pltpu.VMEM((N, ROWS_A, 128), BF),
            pltpu.VMEM((N, ROWS_A, 128), BF),
            pltpu.VMEM((N, ROWS_B, 128), BF),
            pltpu.VMEM((N, ROWS_B, 128), BF),
            pltpu.VMEM((N * 8, 512), F32),
            pltpu.VMEM((8, 64, 512), F32),
            pltpu.VMEM((32, 8, 512), F32),
            pltpu.VMEM((64, 512), F32),
            pltpu.VMEM((8, 512), F32),
            pltpu.VMEM((8, 128), F32),
            dma((3,)), dma, dma((4,)), dma, dma((4,)), dma((4,)), dma((4,)),
            dma((4,)), dma((4,)), dma, dma, dma, dma, dma, dma,
        ],
        compiler_params=pltpu.CompilerParams(
            collective_id=0, has_side_effects=True, vmem_limit_bytes=60 * 1024 * 1024
        ),
        name="triples",
    )(
        triplets, occ_energy, vir_energy, vir_energy.reshape(1, V), pair_integrals, k_integrals,
        pair_amplitudes, k_amplitudes,
        jnp.asarray(pack_matrix(), BF), jnp.asarray(unpack_matrix(), BF), jnp.asarray(row_matrix(), BF),
    )
    return energy[0, 0:1], density, vvvo


def solution(mesh):
    return jax.shard_map(
        body,
        mesh=mesh,
        in_specs=(
            P("trip", None),
            P(None, "vir", None, None),
            P("trip", "vir", None, None),
            P(),
            P("trip", None, None, None),
            P(),
            P(),
        ),
        out_specs=(P("trip"), P("vir", None), P("trip", "vir", None, None)),
        check_vma=False,
    )
```

```python
import numpy as np
import jax
import jax.numpy as jnp
from jax import lax
from jax.experimental import pallas as pl
from jax.experimental.pallas import tpu as pltpu
from jax.sharding import PartitionSpec as P

MESH = pl.DeviceIdType.MESH
BF, F32 = jnp.bfloat16, jnp.float32
V = 448
N = 64
L = 7
GROUPS = 4
GD = 16
GR = GD * L
SLOT = 64
ROWS_A, ROWS_B = 96, 80


def pack_matrix():
    m = np.zeros((GD, SLOT, L, GD, L), np.float32)
    for p in range(L):
        for q in range(L):
            for j in range(GD):
                m[j, L * p + q, p, j, q] = 1
    return m.reshape(GD * SLOT, L * GR)


def unpack_matrix():
    m = np.zeros((L, GD, L, GD, SLOT), np.float32)
    for p in range(L):
        for q in range(L):
            for k in range(GD):
                m[q, k, p, k, L * p + q] = 1
    return m.reshape(L * GR, GD * SLOT)


def pack_last():
    m = np.zeros((GD, 8, GD, L), np.float32)
    for j in range(GD):
        m[j, :, j, L - 1] = 1
    return m.reshape(GD * 8, GR)


def unpack_last():
    m = np.zeros((GD, L, GD, 8), np.float32)
    for j in range(GD):
        m[j, L - 1, j, 0] = 1
    return m.reshape(GR, GD * 8)


def row_matrix():
    m = np.zeros((N, 8, N, L), np.float32)
    for j in range(N):
        for i in range(L):
            m[j, i, j, i] = 1
    return m.reshape(N * 8, V)


def nn(x, y):
    return lax.dot_general(x, y, (((1,), (0,)), ((), ())), preferred_element_type=F32)


def nt(x, y):
    return lax.dot_general(x, y, (((1,), (1,)), ((), ())), preferred_element_type=F32)


def tn(x, y):
    return lax.dot_general(x, y, (((0,), (0,)), ((), ())), preferred_element_type=F32)


def iota(shape, dim):
    return lax.broadcasted_iota(jnp.int32, shape, dim)


def packed_a(x, pk):
    o = nn(pk[...], x).reshape(GD, SLOT, 256)
    return o[:, :48, :128].astype(BF), o[:, :48, 128:].astype(BF)


def packed_b(x, last, pk, pl_ref):
    o = nn(pk[...], x).reshape(GD, SLOT, 256)
    t = nn(pl_ref[...], last).reshape(GD, 8, 256)
    shape = (GD, 32, 128)
    row = iota(shape, 1)
    r0 = jnp.broadcast_to(t[:, 0:1, :128], shape)
    r1 = jnp.broadcast_to(t[:, 0:1, 128:], shape)
    r2 = jnp.broadcast_to(o[:, 48:49, :128], shape)
    high = jnp.where(row == 24, r0, jnp.where(row == 26, r1, jnp.where(row == 30, r2, o[:, 32:64, 128:])))
    high = pltpu.roll(high, 64, 2)
    high = jnp.where(row == 25, r0, jnp.where(row == 27, r1, jnp.where(row == 31, r2, high)))
    mixed = jnp.where(iota(shape, 2) < 64, o[:, :32, 128:], high)
    return o[:, :48, :128].astype(BF), mixed.astype(BF)


def spread_a(m0, m1, tmp):
    zero = jnp.zeros((GD, 16, 128), BF)
    tmp[:, 0:128] = jnp.concatenate([m0, zero], axis=1).reshape(GD * SLOT, 128)
    tmp[:, 128:256] = jnp.concatenate([m1, zero], axis=1).reshape(GD * SLOT, 128)


def spread_b(m0, mixed, tmp):
    mixed = mixed.astype(F32)
    lane = iota((GD, 32, 128), 2) < 64
    turned = pltpu.roll(mixed, 64, 2)
    low = jnp.where(lane, mixed, 0.0).astype(BF)
    high = jnp.where(lane, turned, 0.0).astype(BF)

    def joined(k, rows):
        row = jnp.where(
            iota((GD, 1, 128), 2) < 64, turned[:, k : k + 1, :], mixed[:, k + 1 : k + 2, :]
        )
        return jnp.broadcast_to(row, (GD, rows, 128))

    full = joined(30, 16).astype(BF)
    tmp[:, 0:128] = jnp.concatenate([m0, full], axis=1).reshape(GD * SLOT, 128)
    tmp[:, 128:256] = jnp.concatenate([low, high], axis=1).reshape(GD * SLOT, 128)
    return jnp.concatenate(
        [joined(24, 8).reshape(GD * 8, 128), joined(26, 8).reshape(GD * 8, 128)], axis=1
    ).astype(BF)


def kernel(
    trip_ref, occ_ref, virs_ref, vir_ref, pair_hbm, k_hbm, tij_hbm, kamp_hbm, pk_hbm, up_hbm, row_hbm, plast, ulast,
    energy_ref, density_ref, vvvo_hbm,
    gi, gj, gk, tij, kamp, pk, up, rowm, cs, w, xb, tjt, tit, vrow, tmp,
    g_send, g_recv, sa_send, sa_recv, sb_send, sb_recv, ya_send, ya_recv, yb_send, yb_recv,
    gram, d1, d2, d2s, dfin,
    ld, g_ss, g_zs, y_ss, y_fs, y_l, y_r, y_o, a_ss, a_rs, d1_ss, d1_rs, d2_ss, d2_rs, d3_ss, d3_rs,
):
    v = lax.axis_index("vir")
    y = lax.axis_index("trip")
    core = lax.rem(v, 2)
    grp = v // GD
    inner = lax.rem(v, GD)
    chip = v // 2

    loads = [
        pltpu.make_async_copy(src, dst, ld.at[n])
        for n, (src, dst) in enumerate(
            (
                (pk_hbm, pk), (pair_hbm.at[1], gj), (k_hbm.at[0], gk), (tij_hbm, tij),
                (pair_hbm.at[0], gi), (kamp_hbm, kamp), (up_hbm, up), (row_hbm, rowm),
            )
        )
    ]
    for n in range(2):
        loads[n].start()

    barrier = pltpu.get_barrier_semaphore()

    def greet(k, c):
        pl.semaphore_signal(
            barrier, inc=1, device_id={"vir": lax.rem(v + k, N), "trip": y}, device_id_type=MESH
        )
        return c

    lax.fori_loop(1, N, greet, 0)
    partner = chip * 2 + (1 - core)
    for dy in (1, 2, 3):
        ty = lax.rem(y + dy, 4)
        pl.semaphore_signal(barrier, inc=1, device_id={"vir": v, "trip": ty}, device_id_type=MESH)
        pl.semaphore_signal(
            barrier, inc=1, device_id={"vir": partner, "trip": ty}, device_id_type=MESH
        )

    for n in range(2):
        loads[n].wait()
    for n in range(2, 8):
        loads[n].start()

    def send_group(src, dst, g, ss, rs):
        def one(k, c):
            d = g * GD + lax.rem(inner + k, GD)

            @pl.when(d != v)
            def _():
                pltpu.make_async_remote_copy(
                    src_ref=src.at[d], dst_ref=dst.at[v], send_sem=ss, recv_sem=rs,
                    device_id={"vir": d, "trip": y}, device_id_type=MESH,
                ).start()

            @pl.when(d == v)
            def _():
                pltpu.make_async_copy(src.at[d], dst.at[v], rs).start()

            return c

        lax.fori_loop(0, GD, one, 0)

    def rows_of(g):
        return pl.ds(pl.multiple_of(g * GR, 16), GR)

    def slots_of(g):
        return pl.ds(g * GD, GD)

    def turn(s, c):
        g = lax.rem(grp + s, GROUPS)
        x = gj[:, rows_of(g), 0:256].reshape(L * GR, 256)
        m0, m1 = packed_a(x, pk)
        g_send[0, slots_of(g)] = m0
        g_send[1, slots_of(g)] = m1
        z = jnp.concatenate([gj[:, rows_of(g), 256:V], jnp.zeros((L, GR, 64), BF)], axis=2)
        m0, mixed = packed_b(z.reshape(L * GR, 256), gj[L - 1, rows_of(g), 0:256], pk, plast)
        g_send[3, slots_of(g)] = m0
        g_send[2, slots_of(g), 0:32] = mixed

        @pl.when(s == 0)
        def _():
            pl.semaphore_wait(barrier, N - 1 + 6)

        @pl.when(y != 2)
        def _():
            send_group(g_send.at[y], g_recv.at[y], g, g_ss, g_zs.at[grp])

        @pl.when(y == 2)
        def _():
            send_group(
                g_send.at[2, :, pl.ds(0, 32)], g_recv.at[2, :, pl.ds(0, 32)], g, g_ss, g_zs.at[grp]
            )

        return c

    lax.fori_loop(0, GROUPS, turn, 0)

    up_y, down_y = lax.rem(y + 1, 4), lax.rem(y + 3, 4)
    far_y = lax.rem(y + 2, 4)

    def by_size(q, act):
        @pl.when(q != 2)
        def _():
            act(48)

        @pl.when(q == 2)
        def _():
            act(32)

    def y_copy(q, s, rows, ty, rs, ss=None):
        g = lax.rem(grp + GROUPS - s, GROUPS)
        piece = g_recv.at[q, slots_of(g), pl.ds(0, rows)]
        return pltpu.make_async_remote_copy(
            src_ref=piece, dst_ref=piece,
            send_sem=y_ss.at[s] if ss is None else ss, recv_sem=rs,
            device_id={"vir": v, "trip": ty}, device_id_type=MESH,
        )

    def z_step(s):
        g = lax.rem(grp + GROUPS - s, GROUPS)

        def act(rows):
            y_copy(y, s, rows, up_y, g_zs.at[g]).wait_recv()
            y_copy(y, s, rows, up_y, y_l.at[s]).start()
            y_copy(y, s, rows, down_y, y_r.at[s]).start()

        by_size(y, act)

    def y_step(s):
        def left(rows):
            y_copy(down_y, s, rows, up_y, y_l.at[s]).wait_recv()
            if s % 2 == 0:
                y_copy(down_y, s, rows, up_y, y_o.at[s], y_fs.at[s]).start()

        def right(rows):
            y_copy(up_y, s, rows, up_y, y_r.at[s]).wait_recv()
            if s % 2 == 1:
                y_copy(up_y, s, rows, down_y, y_o.at[s], y_fs.at[s]).start()

        by_size(down_y, left)
        by_size(up_y, right)

    def far_step(s):
        by_size(far_y, lambda rows: y_copy(far_y, s, rows, up_y, y_o.at[s]).wait_recv())
        g = lax.rem(grp + GROUPS - s, GROUPS)
        last = spread_b(g_recv[3, slots_of(g)], g_recv[2, slots_of(g), 0:32], tmp)
        o = nn(up[...], tmp[...])
        gj[:, rows_of(g), 256:V] = o.reshape(L, GR, 256)[:, :, 0:192].astype(BF)
        spread_a(g_recv[0, slots_of(g)], g_recv[1, slots_of(g)], tmp)
        o = nn(up[...], tmp[...])
        gj[:, rows_of(g), 0:256] = o.reshape(L, GR, 256).astype(BF)
        fix = nn(ulast[...], last)
        gj[L - 1, rows_of(g), 0:256] = (o[GR * (L - 1) :] + fix).astype(BF)

    for n in range(2, 8):
        loads[n].wait()

    def c_part(c, carry):
        x = gk[c]
        cs[c] = nt(tij[...], x) + nn(x, tij[...])
        return carry

    def a_part(i, carry):
        x = gi[i]
        w[i, :, 0:V] = nt(x, kamp[0, 1]) + nt(tjt[...], x)
        return carry

    lax.fori_loop(0, 3, c_part, 0)
    z_step(0)
    lax.fori_loop(3, 6, c_part, 0)
    z_step(1)
    y_step(0)
    lax.fori_loop(6, L, c_part, 0)
    tjt[...] = kamp[0, 1].astype(F32).T.astype(BF)
    tit[...] = kamp[0, 0].astype(F32).T.astype(BF)
    z_step(2)
    y_step(1)
    xb[:, :, 384:512] = jnp.zeros((L, V, 128), BF)
    vrow[...] = jnp.ones_like(vrow)
    vrow[0:1, 0:V] = vir_ref[...]
    z_step(3)
    y_step(2)
    far_step(0)
    w[:, :, 384:512] = jnp.zeros((L, V, 128), F32)
    lax.fori_loop(0, 2, a_part, 0)
    y_step(3)
    far_step(1)
    far_step(2)
    lax.fori_loop(2, 5, a_part, 0)
    far_step(3)

    def send_a(src, dst, n):
        def step(s, c):
            g = lax.rem(grp + s, GROUPS)
            m0, m1 = packed_a(xb[:, rows_of(g), 0:256].reshape(L * GR, 256), pk)
            src[slots_of(g), 0:48] = m0
            src[slots_of(g), 48:96] = m1
            send_group(src, dst, g, a_ss.at[n], a_rs.at[n])
            return c

        lax.fori_loop(0, GROUPS, step, 0)

    def send_b(src, dst, n):
        def step(s, c):
            g = lax.rem(grp + s, GROUPS)
            x = xb[:, rows_of(g), 256:512].reshape(L * GR, 256)
            m0, mixed = packed_b(x, xb[L - 1, rows_of(g), 0:256], pk, plast)
            src[slots_of(g), 0:48] = m0
            src[slots_of(g), 48:80] = mixed
            send_group(src, dst, g, a_ss.at[n], a_rs.at[n])
            return c

        lax.fori_loop(0, GROUPS, step, 0)

    def all_of(src, dst, n):
        return pltpu.make_async_remote_copy(
            src_ref=src, dst_ref=dst, send_sem=a_ss.at[n], recv_sem=a_rs.at[n],
            device_id={"vir": lax.rem(v + 1, N), "trip": y}, device_id_type=MESH,
        )

    def s_a(c, carry):
        xb[c, :, 0:256] = (cs[c, :, 0:256] + nt(kamp[0, 0], gj[c, 0:256])).astype(BF)
        return carry

    lax.fori_loop(0, L, s_a, 0)
    send_a(sa_send, sa_recv, 0)

    def s_b(c, carry):
        xb[c, :, 256:V] = (cs[c, :, 256:V] + nt(kamp[0, 0], gj[c, 256:V])).astype(BF)
        return carry

    lax.fori_loop(0, L, s_b, 0)
    send_b(sb_send, sb_recv, 1)

    def b_part(i, carry):
        w[i, :, 0:V] = w[i, :, 0:V] + nt(tit[...], gj[i])
        return carry

    lax.fori_loop(5, L, a_part, 0)
    lax.fori_loop(0, L, b_part, 0)

    shift = occ_ref[trip_ref[0, 0]] + occ_ref[trip_ref[0, 1]] + occ_ref[trip_ref[0, 2]]
    vcol = jnp.sum(
        jnp.where(iota((V, V), 0) == iota((V, V), 1), vrow[0:1, 0:V], 0.0), axis=1, keepdims=True
    )

    index = iota((V, 1), 0)
    late = (index - 7 * ((index * 9363) >> 16)) == L - 1

    def weigh(i, lanes, mask, e):
        x = w[i, :, lanes]
        den = vcol + (vrow[0:1, lanes] + (virs_ref[v * L + i] - shift))
        z = x / den
        xb[i, :, lanes] = z.astype(BF)
        t = x * z
        if mask is not None:
            t = jnp.where(mask, t, 0.0)
        return e + jnp.sum(t, axis=0, keepdims=True)

    first, rest = slice(0, 256), slice(256, 512)
    all_of(sa_send, sa_recv, 0).wait_recv()

    def add_a(g, c):
        spread_a(sa_recv[slots_of(g), 0:48], sa_recv[slots_of(g), 48:96], tmp)
        o = nn(up[...], tmp[...]).reshape(L, GR, 256)
        w[:, rows_of(g), first] = w[:, rows_of(g), first] + o
        return c

    lax.fori_loop(0, GROUPS, add_a, 0)
    e = jnp.zeros((1, 256), F32)
    e = lax.fori_loop(0, L - 1, lambda i, e: weigh(i, first, None, e), e)
    e = weigh(L - 1, first, jnp.logical_not(late), e)
    send_a(ya_send, ya_recv, 2)

    def gram_a(i, acc):
        x = xb[i, :, first]
        return acc + nt(x, x)

    cs[0] = lax.fori_loop(0, L - 1, gram_a, jnp.zeros((V, V), F32))

    all_of(sb_send, sb_recv, 1).wait_recv()

    def add_b(g, c):
        last = spread_b(sb_recv[slots_of(g), 0:48], sb_recv[slots_of(g), 48:80], tmp)
        o = nn(up[...], tmp[...]).reshape(L, GR, 256)
        w[:, rows_of(g), rest] = w[:, rows_of(g), rest] + o
        w[L - 1, rows_of(g), first] = w[L - 1, rows_of(g), first] + nn(ulast[...], last)
        return c

    lax.fori_loop(0, GROUPS, add_b, 0)
    e = lax.fori_loop(0, L, lambda i, e: weigh(i, rest, None, e), e)
    e = weigh(L - 1, first, late, e)
    send_b(yb_send, yb_recv, 3)

    def gram_b(i, acc):
        x = xb[i, :, rest]
        return acc + nt(x, x)

    x = xb[L - 1, :, first]
    total = lax.fori_loop(0, L, gram_b, cs[0] + nt(x, x))

    hi = total.astype(BF)
    left = total - hi.astype(F32)
    mid = left.astype(BF)
    lo = (left - mid.astype(F32)).astype(BF)
    rows = nn(rowm[...], hi) + nn(rowm[...], mid) + nn(rowm[...], lo)
    energy = jnp.sum(e)
    gram[:, 384:512] = jnp.zeros((N * 8, 128), F32)
    gram[:, 0:V] = rows
    spare = lax.rem(iota((N * 8, 128), 0), 8) == 7
    mine = spare & (iota((N * 8, 128), 1) == y)
    gram[:, 0:128] = jnp.where(mine, energy, gram[:, 0:128])

    piece = y * 2 + core

    def piece_copy(k):
        to = lax.rem(piece + k, 8)
        return pltpu.make_async_remote_copy(
            src_ref=gram.at[pl.ds(pl.multiple_of(to * 64, 64), 64)], dst_ref=d1.at[piece],
            send_sem=d1_ss, recv_sem=d1_rs,
            device_id={"vir": chip * 2 + lax.rem(to, 2), "trip": to // 2}, device_id_type=MESH,
        )

    for k in range(1, 8):
        piece_copy(k).start()
    pltpu.make_async_copy(
        gram.at[pl.ds(pl.multiple_of(piece * 64, 64), 64)], d1.at[piece], d1_rs
    ).start()

    all_of(ya_send, ya_recv, 2).wait_recv()

    def take_a(g, c):
        spread_a(ya_recv[slots_of(g), 0:48], ya_recv[slots_of(g), 48:96], tmp)
        o = nn(up[...], tmp[...]).reshape(L, GR, 256)
        gk[:, rows_of(g), 0:256] = o.astype(BF)
        return c

    lax.fori_loop(0, GROUPS, take_a, 0)

    def out_first(c, carry):
        x = gk[c, :, 0:256]
        cs[c] = nt(x, tij[:, 0:256])
        cs[c, 0:256] = cs[c, 0:256] + tn(x, tij[...])
        return carry

    lax.fori_loop(0, L - 1, out_first, 0)

    pltpu.make_async_copy(d1, d1, d1_rs).wait()
    d2s[...] = jnp.sum(d1[...], axis=0)

    def owner_send(o, c):
        to = piece * 8 + o
        src = d2s.at[pl.ds(pl.multiple_of(o * 8, 8), 8)]

        @pl.when(to != v)
        def _():
            pltpu.make_async_remote_copy(
                src_ref=src, dst_ref=d2.at[chip], send_sem=d2_ss, recv_sem=d2_rs,
                device_id={"vir": to, "trip": y}, device_id_type=MESH,
            ).start()

        @pl.when(to == v)
        def _():
            pltpu.make_async_copy(src, d2.at[chip], d2_rs).start()

        return c

    lax.fori_loop(0, 8, owner_send, 0)

    is_owner = y == grp

    def fin_copy(ty):
        return pltpu.make_async_remote_copy(
            src_ref=dfin, dst_ref=dfin, send_sem=d3_ss, recv_sem=d3_rs,
            device_id={"vir": v, "trip": ty}, device_id_type=MESH,
        )

    all_of(yb_send, yb_recv, 3).wait_recv()

    def take_b(g, c):
        last = spread_b(yb_recv[slots_of(g), 0:48], yb_recv[slots_of(g), 48:80], tmp)
        o = nn(up[...], tmp[...]).reshape(L, GR, 256)
        gk[:, rows_of(g), 256:V] = o[:, :, 0:192].astype(BF)
        fix = gk[L - 1, rows_of(g), first].astype(F32) + nn(ulast[...], last)
        gk[L - 1, rows_of(g), first] = fix.astype(BF)
        return c

    lax.fori_loop(0, GROUPS, take_b, 0)

    @pl.when(is_owner)
    def _():
        pltpu.make_async_copy(d2, d2, d2_rs).wait()
        dfin[...] = jnp.sum(d2[...], axis=0)
        for dy in (1, 2, 3):
            fin_copy(lax.rem(y + dy, 4)).start()

    def out_last(c, carry):
        x = gk[c, :, 256:V]
        acc = cs[c] + nt(x, tij[:, 256:V])
        gi[c, 0:256] = acc[0:256].astype(BF)
        gi[c, 256:V] = (acc[256:V] + tn(x, tij[...])).astype(BF)
        pltpu.make_async_copy(gi.at[c], vvvo_hbm.at[0, c], ld.at[0]).start()
        return carry

    x = gk[L - 1]
    gi[L - 1] = (nt(x, tij[...]) + tn(x, tij[...])).astype(BF)
    pltpu.make_async_copy(gi.at[L - 1], vvvo_hbm.at[0, L - 1], ld.at[0]).start()
    lax.fori_loop(0, L - 1, out_last, 0)

    @pl.when(jnp.logical_not(is_owner))
    def _():
        fin_copy(y).wait_recv()

    density_ref[...] = dfin[0:7, 0:V] * (1.0 / (V * V))
    sel = iota((1, 128), 1) == y
    es = jnp.sum(jnp.where(sel, dfin[7:8, 0:128], 0.0), axis=1, keepdims=True)
    energy_ref[...] = jnp.broadcast_to(es * (1.0 / V**3), (8, 128))

    pltpu.make_async_copy(gi, vvvo_hbm.at[0], ld.at[0]).wait()
    def drain_g(rows):
        part = g_send.at[0, pl.ds(0, N - 1), pl.ds(0, rows)]
        pltpu.make_async_remote_copy(
            src_ref=part, dst_ref=part, send_sem=g_ss, recv_sem=g_ss,
            device_id={"vir": v, "trip": up_y}, device_id_type=MESH,
        ).wait_send()

    by_size(y, drain_g)
    for s in range(GROUPS):

        def drain_y(rows):
            part = g_send.at[0, pl.ds(0, 2 * GD), pl.ds(0, rows)]
            pltpu.make_async_remote_copy(
                src_ref=part, dst_ref=part, send_sem=y_ss.at[s], recv_sem=g_ss,
                device_id={"vir": v, "trip": up_y}, device_id_type=MESH,
            ).wait_send()

        by_size(y, drain_y)
        by_size(
            down_y if s % 2 == 0 else up_y,
            lambda rows: y_copy(y, s, rows, up_y, g_ss, y_fs.at[s]).wait_send(),
        )
    for n, buf in enumerate((sa_send, sb_send, ya_send, yb_send)):
        part = buf.at[pl.ds(0, N - 1)]
        all_of(part, part, n).wait_send()
    part = d1.at[pl.ds(0, 7)]
    pltpu.make_async_remote_copy(
        src_ref=part, dst_ref=part, send_sem=d1_ss, recv_sem=d1_ss,
        device_id={"vir": v, "trip": up_y}, device_id_type=MESH,
    ).wait_send()

    def drain_owner(count):
        q = d2.at[pl.ds(0, count)]
        pltpu.make_async_remote_copy(
            src_ref=q, dst_ref=q, send_sem=d2_ss, recv_sem=d2_ss,
            device_id={"vir": v, "trip": up_y}, device_id_type=MESH,
        ).wait_send()

    own_piece = (v // 8) == piece

    @pl.when(own_piece)
    def _():
        drain_owner(7)

    @pl.when(jnp.logical_not(own_piece))
    def _():
        drain_owner(8)

    @pl.when(is_owner)
    def _():
        for dy in (1, 2, 3):
            fin_copy(lax.rem(y + dy, 4)).wait_send()


def body(triplets, pair_integrals, k_integrals, pair_amplitudes, k_amplitudes, occ_energy, vir_energy):
    vm = pl.BlockSpec(memory_space=pltpu.VMEM)
    sm = pl.BlockSpec(memory_space=pltpu.SMEM)
    hbm = pl.BlockSpec(memory_space=pl.ANY)
    slab = pltpu.VMEM((L, V, V), BF)
    dma = pltpu.SemaphoreType.DMA
    energy, density, vvvo = pl.pallas_call(
        kernel,
        out_shape=(
            jax.ShapeDtypeStruct((8, 128), F32),
            jax.ShapeDtypeStruct((L, V), F32),
            jax.ShapeDtypeStruct((1, L, V, V), BF),
        ),
        in_specs=[sm, sm, sm, vm, hbm, hbm, hbm, hbm, hbm, hbm, hbm, vm, vm],
        out_specs=(vm, vm, hbm),
        scratch_shapes=[
            slab, slab, slab,
            pltpu.VMEM((V, V), BF),
            pltpu.VMEM((1, 2, V, V), BF),
            pltpu.VMEM((GD * SLOT, L * GR), BF),
            pltpu.VMEM((L * GR, GD * SLOT), BF),
            pltpu.VMEM((N * 8, V), BF),
            pltpu.VMEM((L, V, V), F32),
            pltpu.VMEM((L, V, 512), F32),
            pltpu.VMEM((L, V, 512), BF),
            pltpu.VMEM((V, V), BF),
            pltpu.VMEM((V, V), BF),
            pltpu.VMEM((8, 512), F32),
            pltpu.VMEM((GD * SLOT, 256), BF),
            pltpu.VMEM((4, N, 48, 128), BF),
            pltpu.VMEM((4, N, 48, 128), BF),
            pltpu.VMEM((N, ROWS_A, 128), BF),
            pltpu.VMEM((N, ROWS_A, 128), BF),
            pltpu.VMEM((N, ROWS_B, 128), BF),
            pltpu.VMEM((N, ROWS_B, 128), BF),
            pltpu.VMEM((N, ROWS_A, 128), BF),
            pltpu.VMEM((N, ROWS_A, 128), BF),
            pltpu.VMEM((N, ROWS_B, 128), BF),
            pltpu.VMEM((N, ROWS_B, 128), BF),
            pltpu.VMEM((N * 8, 512), F32),
            pltpu.VMEM((8, 64, 512), F32),
            pltpu.VMEM((32, 8, 512), F32),
            pltpu.VMEM((64, 512), F32),
            pltpu.VMEM((8, 512), F32),
            dma((8,)), dma, dma((4,)), dma((4,)), dma((4,)), dma((4,)), dma((4,)), dma((4,)),
            dma((4,)), dma((4,)), dma, dma, dma, dma, dma, dma,
        ],
        compiler_params=pltpu.CompilerParams(
            collective_id=0, has_side_effects=True, vmem_limit_bytes=60 * 1024 * 1024
        ),
        name="triples",
    )(
        triplets, occ_energy, vir_energy, vir_energy.reshape(1, V), pair_integrals, k_integrals,
        pair_amplitudes, k_amplitudes,
        jnp.asarray(pack_matrix(), BF), jnp.asarray(unpack_matrix(), BF), jnp.asarray(row_matrix(), BF),
        jnp.asarray(pack_last(), BF), jnp.asarray(unpack_last(), BF),
    )
    return energy[0, 0:1], density, vvvo


def solution(mesh):
    return jax.shard_map(
        body,
        mesh=mesh,
        in_specs=(
            P("trip", None),
            P(None, "vir", None, None),
            P("trip", "vir", None, None),
            P(),
            P("trip", None, None, None),
            P(),
            P(),
        ),
        out_specs=(P("trip"), P("vir", None), P("trip", "vir", None, None)),
        check_vma=False,
    )
```

```python
import numpy as np
import jax
import jax.numpy as jnp
from jax import lax
from jax.experimental import pallas as pl
from jax.experimental.pallas import tpu as pltpu
from jax.sharding import PartitionSpec as P

MESH = pl.DeviceIdType.MESH
BF, F32 = jnp.bfloat16, jnp.float32
V = 448
N = 64
L = 7
GROUPS = 4
GD = 16
GR = GD * L
SLOT = 64
ROWS_A, ROWS_B = 96, 80


def pack_matrix():
    m = np.zeros((GD, SLOT, L, GD, L), np.float32)
    for p in range(L):
        for q in range(L):
            for j in range(GD):
                m[j, L * p + q, p, j, q] = 1
    return m.reshape(GD * SLOT, L * GR)


def unpack_matrix():
    m = np.zeros((L, GD, L, GD, SLOT), np.float32)
    for p in range(L):
        for q in range(L):
            for k in range(GD):
                m[q, k, p, k, L * p + q] = 1
    return m.reshape(L * GR, GD * SLOT)


def pack_last():
    m = np.zeros((GD, 8, GD, L), np.float32)
    for j in range(GD):
        m[j, :, j, L - 1] = 1
    return m.reshape(GD * 8, GR)


def unpack_last():
    m = np.zeros((GD, L, GD, 8), np.float32)
    for j in range(GD):
        m[j, L - 1, j, 0] = 1
    return m.reshape(GR, GD * 8)


def turn_pack_matrix():
    m = np.zeros((GD, 32, 4, GD, L), np.float32)
    for p in range(4):
        for q in range(L):
            for j in range(GD):
                m[j, L * p + q, p, j, q] = 1
    return m.reshape(GD * 32, 4 * GR)


def turn_unpack_matrix():
    m = np.zeros((L, 4, GD, GD, 32), np.float32)
    for p in range(4):
        for q in range(L):
            for k in range(GD):
                m[q, p, k, k, L * p + q] = 1
    return m.reshape(L * 4 * GD, GD * 32)


def row_matrix():
    m = np.zeros((N, 8, N, L), np.float32)
    for j in range(N):
        for i in range(L):
            m[j, i, j, i] = 1
    return m.reshape(N * 8, V)


def nn(x, y):
    return lax.dot_general(x, y, (((1,), (0,)), ((), ())), preferred_element_type=F32)


def nt(x, y):
    return lax.dot_general(x, y, (((1,), (1,)), ((), ())), preferred_element_type=F32)


def tn(x, y):
    return lax.dot_general(x, y, (((0,), (0,)), ((), ())), preferred_element_type=F32)


def iota(shape, dim):
    return lax.broadcasted_iota(jnp.int32, shape, dim)


def packed_a(x, pk):
    o = nn(pk[...], x).reshape(GD, SLOT, 256)
    return o[:, :48, :128].astype(BF), o[:, :48, 128:].astype(BF)


def packed_b(x, last, pk, pl_ref):
    o = nn(pk[...], x).reshape(GD, SLOT, 256)
    t = nn(pl_ref[...], last).reshape(GD, 8, 256)
    shape = (GD, 32, 128)
    row = iota(shape, 1)
    r0 = jnp.broadcast_to(t[:, 0:1, :128], shape)
    r1 = jnp.broadcast_to(t[:, 0:1, 128:], shape)
    r2 = jnp.broadcast_to(o[:, 48:49, :128], shape)
    high = jnp.where(row == 24, r0, jnp.where(row == 26, r1, jnp.where(row == 30, r2, o[:, 32:64, 128:])))
    high = pltpu.roll(high, 64, 2)
    high = jnp.where(row == 25, r0, jnp.where(row == 27, r1, jnp.where(row == 31, r2, high)))
    mixed = jnp.where(iota(shape, 2) < 64, o[:, :32, 128:], high)
    return o[:, :48, :128].astype(BF), mixed.astype(BF)


def spread_a(m0, m1, tmp):
    zero = jnp.zeros((GD, 16, 128), BF)
    tmp[:, 0:128] = jnp.concatenate([m0, zero], axis=1).reshape(GD * SLOT, 128)
    tmp[:, 128:256] = jnp.concatenate([m1, zero], axis=1).reshape(GD * SLOT, 128)


def spread_b(m0, mixed, tmp):
    mixed = mixed.astype(F32)
    lane = iota((GD, 32, 128), 2) < 64
    turned = pltpu.roll(mixed, 64, 2)
    low = jnp.where(lane, mixed, 0.0).astype(BF)
    high = jnp.where(lane, turned, 0.0).astype(BF)

    def joined(k, rows):
        row = jnp.where(
            iota((GD, 1, 128), 2) < 64, turned[:, k : k + 1, :], mixed[:, k + 1 : k + 2, :]
        )
        return jnp.broadcast_to(row, (GD, rows, 128))

    full = joined(30, 16).astype(BF)
    tmp[:, 0:128] = jnp.concatenate([m0, full], axis=1).reshape(GD * SLOT, 128)
    tmp[:, 128:256] = jnp.concatenate([low, high], axis=1).reshape(GD * SLOT, 128)
    return jnp.concatenate(
        [joined(24, 8).reshape(GD * 8, 128), joined(26, 8).reshape(GD * 8, 128)], axis=1
    ).astype(BF)


def kernel(
    trip_ref, occ_ref, virs_ref, vir_ref, pair_hbm, k_hbm, tij_hbm, kamp_hbm, pk_hbm, up_hbm, row_hbm, plast, ulast, pkt, upt,
    energy_ref, density_ref, vvvo_hbm,
    gi, gj, gk, tij, kamp, pk, up, rowm, cs, w, xb, tjt, tit, tjp, tijp, pm, pmt, vrow, tmp, tmpt,
    g_send, g_recv, sa_send, sa_recv, sb_send, sb_recv, ya_send, ya_recv, yb_send, yb_recv,
    gram, d1, d2, d2s, dfin,
    ld, g_ss, g_zs, y_ss, y_fs, y_l, y_r, y_o, a_ss, a_rs, d1_ss, d1_rs, d2_ss, d2_rs, d3_ss, d3_rs,
):
    v = lax.axis_index("vir")
    y = lax.axis_index("trip")
    core = lax.rem(v, 2)
    grp = v // GD
    inner = lax.rem(v, GD)
    chip = v // 2

    loads = [
        pltpu.make_async_copy(src, dst, ld.at[n])
        for n, (src, dst) in enumerate(
            (
                (pair_hbm.at[1], gj), (k_hbm.at[0], gk), (tij_hbm, tij), (pk_hbm, pk),
                (pair_hbm.at[0], gi), (kamp_hbm, kamp), (up_hbm, up), (row_hbm, rowm),
            )
        )
    ]
    loads[0].start()

    barrier = pltpu.get_barrier_semaphore()

    def greet(k, c):
        pl.semaphore_signal(
            barrier, inc=1, device_id={"vir": lax.rem(v + k, N), "trip": y}, device_id_type=MESH
        )
        return c

    lax.fori_loop(1, N, greet, 0)
    partner = chip * 2 + (1 - core)
    for dy in (1, 2, 3):
        ty = lax.rem(y + dy, 4)
        pl.semaphore_signal(barrier, inc=1, device_id={"vir": v, "trip": ty}, device_id_type=MESH)
        pl.semaphore_signal(
            barrier, inc=1, device_id={"vir": partner, "trip": ty}, device_id_type=MESH
        )

    loads[0].wait()
    for n in range(1, 8):
        loads[n].start()
    xb[:, :, 384:512] = jnp.zeros((L, V, 128), BF)

    def send_group(src, dst, g, ss, rs):
        def one(k, c):
            d = g * GD + lax.rem(inner + k, GD)

            @pl.when(d != v)
            def _():
                pltpu.make_async_remote_copy(
                    src_ref=src.at[d], dst_ref=dst.at[v], send_sem=ss, recv_sem=rs,
                    device_id={"vir": d, "trip": y}, device_id_type=MESH,
                ).start()

            @pl.when(d == v)
            def _():
                pltpu.make_async_copy(src.at[d], dst.at[v], rs).start()

            return c

        lax.fori_loop(0, GD, one, 0)

    def rows_of(g):
        return pl.ds(pl.multiple_of(g * GR, 16), GR)

    def slots_of(g):
        return pl.ds(g * GD, GD)

    tile = pl.ds(pl.multiple_of(y * 128, 128), 128)

    def turn(s, c):
        g = lax.rem(grp + s, GROUPS)
        xb[:, rows_of(g), 0:V] = gj[:, rows_of(g), :]
        x = xb[0:4, rows_of(g), tile].reshape(4 * GR, 128)
        g_send[0, slots_of(g)] = nn(pkt[...], x).astype(BF).reshape(GD, 32, 128)

        @pl.when(s == 0)
        def _():
            pl.semaphore_wait(barrier, N - 1 + 6)

        send_group(g_send.at[0], g_recv.at[0, y], g, g_ss.at[0], g_zs.at[grp])
        return c

    def turn_rest(s, c):
        g = lax.rem(grp + s, GROUPS)
        x = xb[4:L, rows_of(g), tile].reshape(3 * GR, 128)
        g_send[1, slots_of(g)] = nn(pkt[:, 0 : 3 * GR], x).astype(BF).reshape(GD, 32, 128)
        send_group(g_send.at[1], g_recv.at[1, y], g, g_ss.at[1], g_zs.at[GROUPS + grp])
        return c

    lax.fori_loop(0, GROUPS, turn, 0)
    lax.fori_loop(0, GROUPS, turn_rest, 0)

    up_y, down_y = lax.rem(y + 1, 4), lax.rem(y + 3, 4)
    far_y = lax.rem(y + 2, 4)

    def group_at(s):
        return lax.rem(grp + GROUPS - s, GROUPS)

    def y_copy(h, q, s, ty, rs, ss):
        piece = g_recv.at[h, q, slots_of(group_at(s))]
        return pltpu.make_async_remote_copy(
            src_ref=piece, dst_ref=piece, send_sem=ss.at[GROUPS * h + s],
            recv_sem=rs, device_id={"vir": v, "trip": ty}, device_id_type=MESH,
        )

    def z_step(h, s):
        y_copy(h, y, s, up_y, g_zs.at[GROUPS * h + group_at(s)], y_ss).wait_recv()
        y_copy(h, y, s, up_y, y_l.at[GROUPS * h + s], y_ss).start()
        y_copy(h, y, s, down_y, y_r.at[GROUPS * h + s], y_ss).start()

    def y_step(h, s):
        n = GROUPS * h + s
        y_copy(h, down_y, s, up_y, y_l.at[n], y_ss).wait_recv()
        if s % 2 == 0:
            y_copy(h, down_y, s, up_y, y_o.at[n], y_fs).start()
        y_copy(h, up_y, s, up_y, y_r.at[n], y_ss).wait_recv()
        if s % 2 == 1:
            y_copy(h, up_y, s, down_y, y_o.at[n], y_fs).start()

    def far_step(h, s):
        y_copy(h, far_y, s, up_y, y_o.at[GROUPS * h + s], y_ss).wait_recv()
        g = group_at(s)
        for t in range(4):
            tmpt[:, 128 * t : 128 * t + 128] = g_recv[h, t, slots_of(g)].reshape(GD * 32, 128)
        o = nn(upt[...], tmpt[...]).astype(BF)
        for q in range(L):
            for p in range(4 - h):
                at = pl.ds(pl.multiple_of(64 * (4 * h + p) + GD * g, GD), GD)
                gj[q, at, :] = o[GD * (4 * q + p) : GD * (4 * q + p + 1), 0:V]

    pm[...] = jnp.where(
        iota((V, V), 1) == 7 * (iota((V, V), 0) & 63) + (iota((V, V), 0) >> 6), 1.0, 0.0
    ).astype(BF)
    pmt[...] = jnp.where(
        iota((V, V), 0) == 7 * (iota((V, V), 1) & 63) + (iota((V, V), 1) >> 6), 1.0, 0.0
    ).astype(BF)
    for n in range(1, 3):
        loads[n].wait()
    tijp[...] = nt(tij[...], pm[...]).astype(BF)

    def c_part(c, carry):
        x = gk[c]
        cs[c] = nt(tij[...], nn(pm[...], x).astype(BF)) + nn(x, tijp[...])
        return carry

    def a_part(i, carry):
        x = gi[i]
        w[i, :, 0:V] = nt(x, tjp[...]) + nt(tjt[...], nn(pm[...], x).astype(BF))
        return carry

    lax.fori_loop(0, 3, c_part, 0)
    z_step(0, 0)
    lax.fori_loop(3, 6, c_part, 0)
    z_step(0, 1)
    y_step(0, 0)
    lax.fori_loop(6, L, c_part, 0)
    for n in range(3, 8):
        loads[n].wait()
    z_step(0, 2)
    y_step(0, 1)
    z_step(0, 3)
    y_step(0, 2)
    z_step(1, 0)
    far_step(0, 0)
    y_step(0, 3)
    z_step(1, 1)
    far_step(0, 1)
    far_step(0, 2)
    z_step(1, 2)
    far_step(0, 3)
    z_step(1, 3)
    y_step(1, 0)

    def send_a(src, dst, n):
        def step(s, c):
            g = lax.rem(grp + s, GROUPS)
            m0, m1 = packed_a(xb[:, rows_of(g), 0:256].reshape(L * GR, 256), pk)
            src[slots_of(g), 0:48] = m0
            src[slots_of(g), 48:96] = m1
            send_group(src, dst, g, a_ss.at[n], a_rs.at[n])
            return c

        lax.fori_loop(0, GROUPS, step, 0)

    def send_b(src, dst, n):
        def step(s, c):
            g = lax.rem(grp + s, GROUPS)
            x = xb[:, rows_of(g), 256:512].reshape(L * GR, 256)
            m0, mixed = packed_b(x, xb[L - 1, rows_of(g), 0:256], pk, plast)
            src[slots_of(g), 0:48] = m0
            src[slots_of(g), 48:80] = mixed
            send_group(src, dst, g, a_ss.at[n], a_rs.at[n])
            return c

        lax.fori_loop(0, GROUPS, step, 0)

    def all_of(src, dst, n):
        return pltpu.make_async_remote_copy(
            src_ref=src, dst_ref=dst, send_sem=a_ss.at[n], recv_sem=a_rs.at[n],
            device_id={"vir": lax.rem(v + 1, N), "trip": y}, device_id_type=MESH,
        )

    def s_a(c, carry):
        xb[c, :, 0:256] = (cs[c, :, 0:256] + nt(kamp[0, 0], gj[c, 0:256])).astype(BF)
        return carry

    lax.fori_loop(0, L, s_a, 0)
    send_a(sa_send, sa_recv, 0)

    y_step(1, 1)
    tjt[...] = kamp[0, 1].astype(F32).T.astype(BF)
    tit[...] = kamp[0, 0].astype(F32).T.astype(BF)
    tjp[...] = nn(pm[...], kamp[0, 1]).astype(BF)
    vrow[...] = jnp.ones_like(vrow)
    vcol = jnp.sum(
        jnp.where(iota((V, V), 0) == iota((V, V), 1), vir_ref[...], 0.0), axis=1, keepdims=True
    )
    vrow[0:1, 0:V] = jnp.sum(
        jnp.where(iota((V, V), 0) == 7 * (iota((V, V), 1) & 63) + (iota((V, V), 1) >> 6), vcol, 0.0),
        axis=0, keepdims=True,
    )
    y_step(1, 2)
    far_step(1, 0)
    y_step(1, 3)
    far_step(1, 1)
    far_step(1, 2)
    far_step(1, 3)
    w[:, :, 384:512] = jnp.zeros((L, V, 128), F32)

    def s_b(c, carry):
        xb[c, :, 256:V] = (cs[c, :, 256:V] + nt(kamp[0, 0], gj[c, 256:V])).astype(BF)
        return carry

    lax.fori_loop(0, L, s_b, 0)
    send_b(sb_send, sb_recv, 1)

    def b_part(i, carry):
        w[i, :, 0:V] = w[i, :, 0:V] + nt(tit[...], gj[i])
        return carry

    lax.fori_loop(0, L, a_part, 0)
    lax.fori_loop(0, L, b_part, 0)

    shift = occ_ref[trip_ref[0, 0]] + occ_ref[trip_ref[0, 1]] + occ_ref[trip_ref[0, 2]]
    index = iota((V, 1), 0)
    late = (index - 7 * ((index * 9363) >> 16)) == L - 1

    def weigh(i, lanes, mask, e):
        x = w[i, :, lanes]
        den = vcol + (vrow[0:1, lanes] + (virs_ref[v * L + i] - shift))
        z = x / den
        xb[i, :, lanes] = z.astype(BF)
        t = x * z
        if mask is not None:
            t = jnp.where(mask, t, 0.0)
        return e + jnp.sum(t, axis=0, keepdims=True)

    first, rest = slice(0, 256), slice(256, 512)
    all_of(sa_send, sa_recv, 0).wait_recv()

    def add_a(g, c):
        spread_a(sa_recv[slots_of(g), 0:48], sa_recv[slots_of(g), 48:96], tmp)
        o = nn(up[...], tmp[...]).reshape(L, GR, 256)
        w[:, rows_of(g), first] = w[:, rows_of(g), first] + o
        return c

    lax.fori_loop(0, GROUPS, add_a, 0)
    e = jnp.zeros((1, 256), F32)
    e = lax.fori_loop(0, L - 1, lambda i, e: weigh(i, first, None, e), e)
    e = weigh(L - 1, first, jnp.logical_not(late), e)
    send_a(ya_send, ya_recv, 2)

    def gram_a(i, acc):
        x = xb[i, :, first]
        return acc + nt(x, x)

    cs[0] = lax.fori_loop(0, L - 1, gram_a, jnp.zeros((V, V), F32))

    all_of(sb_send, sb_recv, 1).wait_recv()

    def add_b(g, c):
        last = spread_b(sb_recv[slots_of(g), 0:48], sb_recv[slots_of(g), 48:80], tmp)
        o = nn(up[...], tmp[...]).reshape(L, GR, 256)
        w[:, rows_of(g), rest] = w[:, rows_of(g), rest] + o
        w[L - 1, rows_of(g), first] = w[L - 1, rows_of(g), first] + nn(ulast[...], last)
        return c

    lax.fori_loop(0, GROUPS, add_b, 0)
    e = lax.fori_loop(0, L, lambda i, e: weigh(i, rest, None, e), e)
    e = weigh(L - 1, first, late, e)
    send_b(yb_send, yb_recv, 3)

    def gram_b(i, acc):
        x = xb[i, :, rest]
        return acc + nt(x, x)

    x = xb[L - 1, :, first]
    total = lax.fori_loop(0, L, gram_b, cs[0] + nt(x, x))

    hi = total.astype(BF)
    left = total - hi.astype(F32)
    mid = left.astype(BF)
    lo = (left - mid.astype(F32)).astype(BF)
    rows = nn(rowm[...], hi) + nn(rowm[...], mid) + nn(rowm[...], lo)
    energy = jnp.sum(e)
    gram[:, 384:512] = jnp.zeros((N * 8, 128), F32)
    gram[:, 0:V] = rows
    spare = lax.rem(iota((N * 8, 128), 0), 8) == 7
    mine = spare & (iota((N * 8, 128), 1) == y)
    gram[:, 0:128] = jnp.where(mine, energy, gram[:, 0:128])

    piece = y * 2 + core

    def piece_copy(k):
        to = lax.rem(piece + k, 8)
        return pltpu.make_async_remote_copy(
            src_ref=gram.at[pl.ds(pl.multiple_of(to * 64, 64), 64)], dst_ref=d1.at[piece],
            send_sem=d1_ss, recv_sem=d1_rs,
            device_id={"vir": chip * 2 + lax.rem(to, 2), "trip": to // 2}, device_id_type=MESH,
        )

    for k in range(1, 8):
        piece_copy(k).start()
    pltpu.make_async_copy(
        gram.at[pl.ds(pl.multiple_of(piece * 64, 64), 64)], d1.at[piece], d1_rs
    ).start()

    all_of(ya_send, ya_recv, 2).wait_recv()

    def take_a(g, c):
        spread_a(ya_recv[slots_of(g), 0:48], ya_recv[slots_of(g), 48:96], tmp)
        o = nn(up[...], tmp[...]).reshape(L, GR, 256)
        gk[:, rows_of(g), 0:256] = o.astype(BF)
        return c

    lax.fori_loop(0, GROUPS, take_a, 0)

    def out_first(c, carry):
        x = gk[c, :, 0:256]
        r = tn(x, tij[...])
        top = r.astype(BF)
        low = (r - top.astype(F32)).astype(BF)
        cs[c] = nt(x, tijp[:, 0:256]) + (nn(pmt[:, 0:256], top) + nn(pmt[:, 0:256], low))
        return carry

    lax.fori_loop(0, L - 1, out_first, 0)

    pltpu.make_async_copy(d1, d1, d1_rs).wait()
    d2s[...] = jnp.sum(d1[...], axis=0)

    def owner_send(o, c):
        to = piece * 8 + o
        src = d2s.at[pl.ds(pl.multiple_of(o * 8, 8), 8)]

        @pl.when(to != v)
        def _():
            pltpu.make_async_remote_copy(
                src_ref=src, dst_ref=d2.at[chip], send_sem=d2_ss, recv_sem=d2_rs,
                device_id={"vir": to, "trip": y}, device_id_type=MESH,
            ).start()

        @pl.when(to == v)
        def _():
            pltpu.make_async_copy(src, d2.at[chip], d2_rs).start()

        return c

    lax.fori_loop(0, 8, owner_send, 0)

    is_owner = y == grp

    def fin_copy(ty):
        return pltpu.make_async_remote_copy(
            src_ref=dfin, dst_ref=dfin, send_sem=d3_ss, recv_sem=d3_rs,
            device_id={"vir": v, "trip": ty}, device_id_type=MESH,
        )

    all_of(yb_send, yb_recv, 3).wait_recv()

    def take_b(g, c):
        last = spread_b(yb_recv[slots_of(g), 0:48], yb_recv[slots_of(g), 48:80], tmp)
        o = nn(up[...], tmp[...]).reshape(L, GR, 256)
        gk[:, rows_of(g), 256:V] = o[:, :, 0:192].astype(BF)
        fix = gk[L - 1, rows_of(g), first].astype(F32) + nn(ulast[...], last)
        gk[L - 1, rows_of(g), first] = fix.astype(BF)
        return c

    lax.fori_loop(0, GROUPS, take_b, 0)

    @pl.when(is_owner)
    def _():
        pltpu.make_async_copy(d2, d2, d2_rs).wait()
        dfin[...] = jnp.sum(d2[...], axis=0)
        for dy in (1, 2, 3):
            fin_copy(lax.rem(y + dy, 4)).start()

    def out_last(c, carry):
        x = gk[c, :, 256:V]
        r = tn(x, tij[...]).astype(BF)
        gi[c] = (cs[c] + (nt(x, tijp[:, 256:V]) + nn(pmt[:, 256:V], r))).astype(BF)
        pltpu.make_async_copy(gi.at[c], vvvo_hbm.at[0, c], ld.at[0]).start()
        return carry

    x = gk[L - 1]
    r = tn(x, tij[...]).astype(BF)
    gi[L - 1] = (nt(x, tijp[...]) + nn(pmt[...], r)).astype(BF)
    pltpu.make_async_copy(gi.at[L - 1], vvvo_hbm.at[0, L - 1], ld.at[0]).start()
    lax.fori_loop(0, L - 1, out_last, 0)

    @pl.when(jnp.logical_not(is_owner))
    def _():
        fin_copy(y).wait_recv()

    density_ref[...] = dfin[0:7, 0:V] * (1.0 / (V * V))
    sel = iota((1, 128), 1) == y
    es = jnp.sum(jnp.where(sel, dfin[7:8, 0:128], 0.0), axis=1, keepdims=True)
    energy_ref[...] = jnp.broadcast_to(es * (1.0 / V**3), (8, 128))

    pltpu.make_async_copy(gi, vvvo_hbm.at[0], ld.at[0]).wait()
    for h in range(2):
        part = g_send.at[0, pl.ds(0, N - 1)]
        pltpu.make_async_remote_copy(
            src_ref=part, dst_ref=part, send_sem=g_ss.at[h], recv_sem=y_l.at[0],
            device_id={"vir": v, "trip": up_y}, device_id_type=MESH,
        ).wait_send()
        for s in range(GROUPS):
            part = g_send.at[0, pl.ds(0, 2 * GD)]
            pltpu.make_async_remote_copy(
                src_ref=part, dst_ref=part, send_sem=y_ss.at[GROUPS * h + s], recv_sem=y_l.at[0],
                device_id={"vir": v, "trip": up_y}, device_id_type=MESH,
            ).wait_send()
            y_copy(h, y, s, up_y, y_l.at[0], y_fs).wait_send()
    for n, buf in enumerate((sa_send, sb_send, ya_send, yb_send)):
        part = buf.at[pl.ds(0, N - 1)]
        all_of(part, part, n).wait_send()
    part = d1.at[pl.ds(0, 7)]
    pltpu.make_async_remote_copy(
        src_ref=part, dst_ref=part, send_sem=d1_ss, recv_sem=d1_ss,
        device_id={"vir": v, "trip": up_y}, device_id_type=MESH,
    ).wait_send()

    def drain_owner(count):
        q = d2.at[pl.ds(0, count)]
        pltpu.make_async_remote_copy(
            src_ref=q, dst_ref=q, send_sem=d2_ss, recv_sem=d2_ss,
            device_id={"vir": v, "trip": up_y}, device_id_type=MESH,
        ).wait_send()

    own_piece = (v // 8) == piece

    @pl.when(own_piece)
    def _():
        drain_owner(7)

    @pl.when(jnp.logical_not(own_piece))
    def _():
        drain_owner(8)

    @pl.when(is_owner)
    def _():
        for dy in (1, 2, 3):
            fin_copy(lax.rem(y + dy, 4)).wait_send()


def body(triplets, pair_integrals, k_integrals, pair_amplitudes, k_amplitudes, occ_energy, vir_energy):
    vm = pl.BlockSpec(memory_space=pltpu.VMEM)
    sm = pl.BlockSpec(memory_space=pltpu.SMEM)
    hbm = pl.BlockSpec(memory_space=pl.ANY)
    slab = pltpu.VMEM((L, V, V), BF)
    dma = pltpu.SemaphoreType.DMA
    energy, density, vvvo = pl.pallas_call(
        kernel,
        out_shape=(
            jax.ShapeDtypeStruct((8, 128), F32),
            jax.ShapeDtypeStruct((L, V), F32),
            jax.ShapeDtypeStruct((1, L, V, V), BF),
        ),
        in_specs=[sm, sm, sm, vm] + [hbm] * 7 + [vm] * 4,
        out_specs=(vm, vm, hbm),
        scratch_shapes=[
            slab, slab, slab,
            pltpu.VMEM((V, V), BF),
            pltpu.VMEM((1, 2, V, V), BF),
            pltpu.VMEM((GD * SLOT, L * GR), BF),
            pltpu.VMEM((L * GR, GD * SLOT), BF),
            pltpu.VMEM((N * 8, V), BF),
            pltpu.VMEM((L, V, V), F32),
            pltpu.VMEM((L, V, 512), F32),
            pltpu.VMEM((L, V, 512), BF),
        ]
        + [pltpu.VMEM((V, V), BF)] * 6
        + [
            pltpu.VMEM((8, 512), F32),
            pltpu.VMEM((GD * SLOT, 256), BF),
            pltpu.VMEM((GD * 32, 512), BF),
            pltpu.VMEM((2, N, 32, 128), BF),
            pltpu.VMEM((2, 4, N, 32, 128), BF),
            pltpu.VMEM((N, ROWS_A, 128), BF),
            pltpu.VMEM((N, ROWS_A, 128), BF),
            pltpu.VMEM((N, ROWS_B, 128), BF),
            pltpu.VMEM((N, ROWS_B, 128), BF),
            pltpu.VMEM((N, ROWS_A, 128), BF),
            pltpu.VMEM((N, ROWS_A, 128), BF),
            pltpu.VMEM((N, ROWS_B, 128), BF),
            pltpu.VMEM((N, ROWS_B, 128), BF),
            pltpu.VMEM((N * 8, 512), F32),
            pltpu.VMEM((8, 64, 512), F32),
            pltpu.VMEM((32, 8, 512), F32),
            pltpu.VMEM((64, 512), F32),
            pltpu.VMEM((8, 512), F32),
            dma((8,)), dma((2,)), dma((8,)), dma((8,)), dma((8,)), dma((8,)), dma((8,)), dma((8,)),
            dma((4,)), dma((4,)), dma, dma, dma, dma, dma, dma,
        ],
        compiler_params=pltpu.CompilerParams(
            collective_id=0, has_side_effects=True, vmem_limit_bytes=60 * 1024 * 1024
        ),
        name="triples",
    )(
        triplets, occ_energy, vir_energy, vir_energy.reshape(1, V), pair_integrals, k_integrals,
        pair_amplitudes, k_amplitudes,
        jnp.asarray(pack_matrix(), BF), jnp.asarray(unpack_matrix(), BF), jnp.asarray(row_matrix(), BF),
        jnp.asarray(pack_last(), BF), jnp.asarray(unpack_last(), BF),
        jnp.asarray(turn_pack_matrix(), BF), jnp.asarray(turn_unpack_matrix(), BF),
    )
    return energy[0, 0:1], density, vvvo


def solution(mesh):
    return jax.shard_map(
        body,
        mesh=mesh,
        in_specs=(
            P("trip", None),
            P(None, "vir", None, None),
            P("trip", "vir", None, None),
            P(),
            P("trip", None, None, None),
            P(),
            P(),
        ),
        out_specs=(P("trip"), P("vir", None), P("trip", "vir", None, None)),
        check_vma=False,
    )
```

```python
import numpy as np
import jax
import jax.numpy as jnp
from jax import lax
from jax.experimental import pallas as pl
from jax.experimental.pallas import tpu as pltpu
from jax.sharding import PartitionSpec as P

MESH = pl.DeviceIdType.MESH
BF, F32 = jnp.bfloat16, jnp.float32
V = 448
N = 64
L = 7
GROUPS = 4
GD = 16
GR = GD * L
SLOT = 64
ROWS_A, ROWS_B = 96, 80


def pack_matrix():
    m = np.zeros((GD, SLOT, L, GD, L), np.float32)
    for p in range(L):
        for q in range(L):
            for j in range(GD):
                m[j, L * p + q, p, j, q] = 1
    return m.reshape(GD * SLOT, L * GR)


def unpack_matrix():
    m = np.zeros((L, GD, L, GD, SLOT), np.float32)
    for p in range(L):
        for q in range(L):
            for k in range(GD):
                m[q, k, p, k, L * p + q] = 1
    return m.reshape(L * GR, GD * SLOT)


def pack_last():
    m = np.zeros((GD, 8, GD, L), np.float32)
    for j in range(GD):
        m[j, :, j, L - 1] = 1
    return m.reshape(GD * 8, GR)


def unpack_last():
    m = np.zeros((GD, L, GD, 8), np.float32)
    for j in range(GD):
        m[j, L - 1, j, 0] = 1
    return m.reshape(GR, GD * 8)


def turn_pack_matrix():
    m = np.zeros((GD, 32, 4, GD, L), np.float32)
    for p in range(4):
        for q in range(L):
            for j in range(GD):
                m[j, L * p + q, p, j, q] = 1
    return m.reshape(GD * 32, 4 * GR)


def turn_unpack_matrix():
    m = np.zeros((L, 4, GD, GD, 32), np.float32)
    for p in range(4):
        for q in range(L):
            for k in range(GD):
                m[q, p, k, k, L * p + q] = 1
    return m.reshape(L * 4 * GD, GD * 32)


def row_matrix():
    m = np.zeros((N, 8, N, L), np.float32)
    for j in range(N):
        for i in range(L):
            m[j, i, j, i] = 1
    return m.reshape(N * 8, V)


def nn(x, y):
    return lax.dot_general(x, y, (((1,), (0,)), ((), ())), preferred_element_type=F32)


def nt(x, y):
    return lax.dot_general(x, y, (((1,), (1,)), ((), ())), preferred_element_type=F32)


def tn(x, y):
    return lax.dot_general(x, y, (((0,), (0,)), ((), ())), preferred_element_type=F32)


def iota(shape, dim):
    return lax.broadcasted_iota(jnp.int32, shape, dim)


def packed_a(x, pk):
    o = nn(pk[...], x).reshape(GD, SLOT, 256)
    return o[:, :48, :128].astype(BF), o[:, :48, 128:].astype(BF)


def packed_b(x, last, pk, pl_ref):
    o = nn(pk[...], x).reshape(GD, SLOT, 256)
    t = nn(pl_ref[...], last).reshape(GD, 8, 256)
    shape = (GD, 32, 128)
    row = iota(shape, 1)
    r0 = jnp.broadcast_to(t[:, 0:1, :128], shape)
    r1 = jnp.broadcast_to(t[:, 0:1, 128:], shape)
    r2 = jnp.broadcast_to(o[:, 48:49, :128], shape)
    high = jnp.where(row == 24, r0, jnp.where(row == 26, r1, jnp.where(row == 30, r2, o[:, 32:64, 128:])))
    high = pltpu.roll(high, 64, 2)
    high = jnp.where(row == 25, r0, jnp.where(row == 27, r1, jnp.where(row == 31, r2, high)))
    mixed = jnp.where(iota(shape, 2) < 64, o[:, :32, 128:], high)
    return o[:, :48, :128].astype(BF), mixed.astype(BF)


def spread_a(m0, m1, tmp):
    zero = jnp.zeros((GD, 16, 128), BF)
    tmp[:, 0:128] = jnp.concatenate([m0, zero], axis=1).reshape(GD * SLOT, 128)
    tmp[:, 128:256] = jnp.concatenate([m1, zero], axis=1).reshape(GD * SLOT, 128)


def spread_b(m0, mixed, tmp):
    mixed = mixed.astype(F32)
    lane = iota((GD, 32, 128), 2) < 64
    turned = pltpu.roll(mixed, 64, 2)
    low = jnp.where(lane, mixed, 0.0).astype(BF)
    high = jnp.where(lane, turned, 0.0).astype(BF)

    def joined(k, rows):
        row = jnp.where(
            iota((GD, 1, 128), 2) < 64, turned[:, k : k + 1, :], mixed[:, k + 1 : k + 2, :]
        )
        return jnp.broadcast_to(row, (GD, rows, 128))

    full = joined(30, 16).astype(BF)
    tmp[:, 0:128] = jnp.concatenate([m0, full], axis=1).reshape(GD * SLOT, 128)
    tmp[:, 128:256] = jnp.concatenate([low, high], axis=1).reshape(GD * SLOT, 128)
    return jnp.concatenate(
        [joined(24, 8).reshape(GD * 8, 128), joined(26, 8).reshape(GD * 8, 128)], axis=1
    ).astype(BF)


def kernel(
    trip_ref, occ_ref, virs_ref, vir_ref, pair_hbm, k_hbm, tij_hbm, kamp_hbm, pk_hbm, up_hbm, row_hbm, plast, ulast, pkt, upt,
    small, cs_hbm, xo_hbm, dx_hbm, tijp_hbm, pmt_hbm,
    gi, gj, gk, tij, kamp, pk, up, rowm, cs, w, xb, tjt, tit, tjp, tijp, pm, pmt, vrow, tmp, tmpt,
    g_send, g_recv, sa_send, sa_recv, sb_send, sb_recv, ya_send, ya_recv, yb_send, yb_recv,
    gram, d1, d2, d2s, dfin,
    ld, g_ss, g_zs, y_ss, y_fs, y_l, y_r, y_o, a_ss, a_rs, yb_rs, d1_ss, d1_rs, d2_ss, d2_rs, d3_ss, d3_rs,
):
    v = lax.axis_index("vir")
    y = lax.axis_index("trip")
    core = lax.rem(v, 2)
    grp = v // GD
    inner = lax.rem(v, GD)
    chip = v // 2

    loads = [
        pltpu.make_async_copy(src, dst, ld.at[n])
        for n, (src, dst) in enumerate(
            (
                (pair_hbm.at[1], gj), (k_hbm.at[0], gk), (tij_hbm, tij), (pk_hbm, pk),
                (pair_hbm.at[0], gi), (kamp_hbm, kamp), (up_hbm, up), (row_hbm, rowm),
            )
        )
    ]
    loads[0].start()

    barrier = pltpu.get_barrier_semaphore()

    def greet(k, c):
        pl.semaphore_signal(
            barrier, inc=1, device_id={"vir": lax.rem(v + k, N), "trip": y}, device_id_type=MESH
        )
        return c

    lax.fori_loop(1, N, greet, 0)
    partner = chip * 2 + (1 - core)
    for dy in (1, 2, 3):
        ty = lax.rem(y + dy, 4)
        pl.semaphore_signal(barrier, inc=1, device_id={"vir": v, "trip": ty}, device_id_type=MESH)
        pl.semaphore_signal(
            barrier, inc=1, device_id={"vir": partner, "trip": ty}, device_id_type=MESH
        )

    loads[0].wait()
    for n in range(1, 8):
        loads[n].start()
    xb[:, :, 384:512] = jnp.zeros((L, V, 128), BF)

    def send_group(src, dst, g, ss, rs):
        def one(k, c):
            d = g * GD + lax.rem(inner + k, GD)

            @pl.when(d != v)
            def _():
                pltpu.make_async_remote_copy(
                    src_ref=src.at[d], dst_ref=dst.at[v], send_sem=ss, recv_sem=rs,
                    device_id={"vir": d, "trip": y}, device_id_type=MESH,
                ).start()

            @pl.when(d == v)
            def _():
                pltpu.make_async_copy(src.at[d], dst.at[v], rs).start()

            return c

        lax.fori_loop(0, GD, one, 0)

    def rows_of(g):
        return pl.ds(pl.multiple_of(g * GR, 16), GR)

    def slots_of(g):
        return pl.ds(g * GD, GD)

    tile = pl.ds(pl.multiple_of(y * 128, 128), 128)

    def turn(s, c):
        g = lax.rem(grp + s, GROUPS)
        xb[:, rows_of(g), 0:V] = gj[:, rows_of(g), :]
        x = xb[0:4, rows_of(g), tile].reshape(4 * GR, 128)
        g_send[0, slots_of(g)] = nn(pkt[...], x).astype(BF).reshape(GD, 32, 128)

        @pl.when(s == 0)
        def _():
            pl.semaphore_wait(barrier, N - 1 + 6)

        send_group(g_send.at[0], g_recv.at[0, y], g, g_ss.at[0], g_zs.at[grp])
        return c

    def turn_rest(s, c):
        g = lax.rem(grp + s, GROUPS)
        x = xb[4:L, rows_of(g), tile].reshape(3 * GR, 128)
        g_send[1, slots_of(g)] = nn(pkt[:, 0 : 3 * GR], x).astype(BF).reshape(GD, 32, 128)
        send_group(g_send.at[1], g_recv.at[1, y], g, g_ss.at[1], g_zs.at[GROUPS + grp])
        return c

    lax.fori_loop(0, GROUPS, turn, 0)
    lax.fori_loop(0, GROUPS, turn_rest, 0)

    up_y, down_y = lax.rem(y + 1, 4), lax.rem(y + 3, 4)
    far_y = lax.rem(y + 2, 4)

    def group_at(s):
        return lax.rem(grp + GROUPS - s, GROUPS)

    def y_copy(h, q, s, ty, rs, ss):
        piece = g_recv.at[h, q, slots_of(group_at(s))]
        return pltpu.make_async_remote_copy(
            src_ref=piece, dst_ref=piece, send_sem=ss.at[GROUPS * h + s],
            recv_sem=rs, device_id={"vir": v, "trip": ty}, device_id_type=MESH,
        )

    def z_step(h, s):
        y_copy(h, y, s, up_y, g_zs.at[GROUPS * h + group_at(s)], y_ss).wait_recv()
        y_copy(h, y, s, up_y, y_l.at[GROUPS * h + s], y_ss).start()
        y_copy(h, y, s, down_y, y_r.at[GROUPS * h + s], y_ss).start()

    def y_step(h, s):
        n = GROUPS * h + s
        y_copy(h, down_y, s, up_y, y_l.at[n], y_ss).wait_recv()
        if s % 2 == 0:
            y_copy(h, down_y, s, up_y, y_o.at[n], y_fs).start()
        y_copy(h, up_y, s, up_y, y_r.at[n], y_ss).wait_recv()
        if s % 2 == 1:
            y_copy(h, up_y, s, down_y, y_o.at[n], y_fs).start()

    def far_step(h, s):
        y_copy(h, far_y, s, up_y, y_o.at[GROUPS * h + s], y_ss).wait_recv()
        g = group_at(s)
        for t in range(4):
            tmpt[:, 128 * t : 128 * t + 128] = g_recv[h, t, slots_of(g)].reshape(GD * 32, 128)
        o = nn(upt[...], tmpt[...]).astype(BF)
        for q in range(L):
            for p in range(4 - h):
                at = pl.ds(pl.multiple_of(64 * (4 * h + p) + GD * g, GD), GD)
                gj[q, at, :] = o[GD * (4 * q + p) : GD * (4 * q + p + 1), 0:V]

    pm[...] = jnp.where(
        iota((V, V), 1) == 7 * (iota((V, V), 0) & 63) + (iota((V, V), 0) >> 6), 1.0, 0.0
    ).astype(BF)
    pmt[...] = jnp.where(
        iota((V, V), 0) == 7 * (iota((V, V), 1) & 63) + (iota((V, V), 1) >> 6), 1.0, 0.0
    ).astype(BF)
    for n in range(1, 3):
        loads[n].wait()
    tijp[...] = nt(tij[...], pm[...]).astype(BF)
    out_t = pltpu.make_async_copy(tijp, tijp_hbm, ld.at[0])
    out_p = pltpu.make_async_copy(pmt, pmt_hbm, ld.at[1])
    out_t.start()
    out_p.start()

    def c_part(c, carry):
        x = gk[c]
        cs[c] = nt(tij[...], nn(pm[...], x).astype(BF)) + nn(x, tijp[...])
        return carry

    def a_part(i, carry):
        x = gi[i]
        w[i, :, 0:V] = nt(x, tjp[...]) + nt(tjt[...], nn(pm[...], x).astype(BF))
        return carry

    lax.fori_loop(0, 3, c_part, 0)
    z_step(0, 0)
    lax.fori_loop(3, 6, c_part, 0)
    z_step(0, 1)
    y_step(0, 0)
    lax.fori_loop(6, L, c_part, 0)
    for n in range(3, 8):
        loads[n].wait()
    z_step(0, 2)
    y_step(0, 1)
    z_step(0, 3)
    y_step(0, 2)
    z_step(1, 0)
    far_step(0, 0)
    y_step(0, 3)
    z_step(1, 1)
    far_step(0, 1)
    far_step(0, 2)
    z_step(1, 2)
    far_step(0, 3)
    z_step(1, 3)
    y_step(1, 0)

    def send_a(src, dst, n):
        def step(s, c):
            g = lax.rem(grp + s, GROUPS)
            m0, m1 = packed_a(xb[:, rows_of(g), 0:256].reshape(L * GR, 256), pk)
            src[slots_of(g), 0:48] = m0
            src[slots_of(g), 48:96] = m1
            send_group(src, dst, g, a_ss.at[n], a_rs.at[n])
            return c

        lax.fori_loop(0, GROUPS, step, 0)

    def send_b(src, dst, n, rs):
        def step(s, c):
            g = lax.rem(grp + s, GROUPS)
            x = xb[:, rows_of(g), 256:512].reshape(L * GR, 256)
            m0, mixed = packed_b(x, xb[L - 1, rows_of(g), 0:256], pk, plast)
            src[slots_of(g), 0:48] = m0
            src[slots_of(g), 48:80] = mixed
            send_group(src, dst, g, a_ss.at[n], rs)
            return c

        lax.fori_loop(0, GROUPS, step, 0)

    def all_of(src, dst, n):
        return pltpu.make_async_remote_copy(
            src_ref=src, dst_ref=dst, send_sem=a_ss.at[n], recv_sem=a_rs.at[n],
            device_id={"vir": lax.rem(v + 1, N), "trip": y}, device_id_type=MESH,
        )

    def s_a(c, carry):
        xb[c, :, 0:256] = (cs[c, :, 0:256] + nt(kamp[0, 0], gj[c, 0:256])).astype(BF)
        return carry

    lax.fori_loop(0, L, s_a, 0)
    send_a(sa_send, sa_recv, 0)

    y_step(1, 1)
    tjt[...] = kamp[0, 1].astype(F32).T.astype(BF)
    tit[...] = kamp[0, 0].astype(F32).T.astype(BF)
    tjp[...] = nn(pm[...], kamp[0, 1]).astype(BF)
    vrow[...] = jnp.ones_like(vrow)
    vcol = jnp.sum(
        jnp.where(iota((V, V), 0) == iota((V, V), 1), vir_ref[...], 0.0), axis=1, keepdims=True
    )
    vrow[0:1, 0:V] = jnp.sum(
        jnp.where(iota((V, V), 0) == 7 * (iota((V, V), 1) & 63) + (iota((V, V), 1) >> 6), vcol, 0.0),
        axis=0, keepdims=True,
    )
    y_step(1, 2)
    far_step(1, 0)
    y_step(1, 3)
    far_step(1, 1)
    far_step(1, 2)
    far_step(1, 3)
    w[:, :, 384:512] = jnp.zeros((L, V, 128), F32)

    def s_b(c, carry):
        xb[c, :, 256:V] = (cs[c, :, 256:V] + nt(kamp[0, 0], gj[c, 256:V])).astype(BF)
        return carry

    lax.fori_loop(0, L, s_b, 0)
    send_b(sb_send, sb_recv, 1, a_rs.at[1])

    def b_part(i, carry):
        w[i, :, 0:V] = w[i, :, 0:V] + nt(tit[...], gj[i])
        return carry

    lax.fori_loop(0, L, a_part, 0)
    lax.fori_loop(0, L, b_part, 0)

    shift = occ_ref[trip_ref[0, 0]] + occ_ref[trip_ref[0, 1]] + occ_ref[trip_ref[0, 2]]
    index = iota((V, 1), 0)
    late = (index - 7 * ((index * 9363) >> 16)) == L - 1

    def weigh(i, lanes, mask, e):
        x = w[i, :, lanes]
        den = vcol + (vrow[0:1, lanes] + (virs_ref[v * L + i] - shift))
        z = x / den
        xb[i, :, lanes] = z.astype(BF)
        t = x * z
        if mask is not None:
            t = jnp.where(mask, t, 0.0)
        return e + jnp.sum(t, axis=0, keepdims=True)

    first, rest = slice(0, 256), slice(256, 512)
    all_of(sa_send, sa_recv, 0).wait_recv()

    def add_a(g, c):
        spread_a(sa_recv[slots_of(g), 0:48], sa_recv[slots_of(g), 48:96], tmp)
        o = nn(up[...], tmp[...]).reshape(L, GR, 256)
        w[:, rows_of(g), first] = w[:, rows_of(g), first] + o
        return c

    lax.fori_loop(0, GROUPS, add_a, 0)
    e = jnp.zeros((1, 256), F32)
    e = lax.fori_loop(0, L - 1, lambda i, e: weigh(i, first, None, e), e)
    e = weigh(L - 1, first, jnp.logical_not(late), e)
    send_a(ya_send, ya_recv, 2)

    def gram_a(i, acc):
        x = xb[i, :, first]
        return acc + nt(x, x)

    cs[0] = lax.fori_loop(0, L - 1, gram_a, jnp.zeros((V, V), F32))

    all_of(sb_send, sb_recv, 1).wait_recv()

    def add_b(g, c):
        last = spread_b(sb_recv[slots_of(g), 0:48], sb_recv[slots_of(g), 48:80], tmp)
        o = nn(up[...], tmp[...]).reshape(L, GR, 256)
        w[:, rows_of(g), rest] = w[:, rows_of(g), rest] + o
        w[L - 1, rows_of(g), first] = w[L - 1, rows_of(g), first] + nn(ulast[...], last)
        return c

    lax.fori_loop(0, GROUPS, add_b, 0)
    e = lax.fori_loop(0, L, lambda i, e: weigh(i, rest, None, e), e)
    e = weigh(L - 1, first, late, e)
    send_b(yb_send, yb_recv, 3, yb_rs.at[grp])

    def gram_b(i, acc):
        x = xb[i, :, rest]
        return acc + nt(x, x)

    x = xb[L - 1, :, first]
    total = lax.fori_loop(0, L, gram_b, cs[0] + nt(x, x))

    hi = total.astype(BF)
    left = total - hi.astype(F32)
    mid = left.astype(BF)
    lo = (left - mid.astype(F32)).astype(BF)
    rows = nn(rowm[...], hi) + nn(rowm[...], mid) + nn(rowm[...], lo)
    energy = jnp.sum(e)
    gram[:, 384:512] = jnp.zeros((N * 8, 128), F32)
    gram[:, 0:V] = rows
    spare = lax.rem(iota((N * 8, 128), 0), 8) == 7
    mine = spare & (iota((N * 8, 128), 1) == y)
    gram[:, 0:128] = jnp.where(mine, energy, gram[:, 0:128])

    piece = y * 2 + core

    def piece_copy(k):
        to = lax.rem(piece + k, 8)
        return pltpu.make_async_remote_copy(
            src_ref=gram.at[pl.ds(pl.multiple_of(to * 64, 64), 64)], dst_ref=d1.at[piece],
            send_sem=d1_ss, recv_sem=d1_rs,
            device_id={"vir": chip * 2 + lax.rem(to, 2), "trip": to // 2}, device_id_type=MESH,
        )

    for k in range(1, 8):
        piece_copy(k).start()
    pltpu.make_async_copy(
        gram.at[pl.ds(pl.multiple_of(piece * 64, 64), 64)], d1.at[piece], d1_rs
    ).start()

    pltpu.make_async_copy(d1, d1, d1_rs).wait()
    d2s[...] = jnp.sum(d1[...], axis=0)

    def owner_send(o, c):
        to = piece * 8 + o
        src = d2s.at[pl.ds(pl.multiple_of(o * 8, 8), 8)]

        @pl.when(to != v)
        def _():
            pltpu.make_async_remote_copy(
                src_ref=src, dst_ref=d2.at[chip], send_sem=d2_ss, recv_sem=d2_rs,
                device_id={"vir": to, "trip": y}, device_id_type=MESH,
            ).start()

        @pl.when(to == v)
        def _():
            pltpu.make_async_copy(src, d2.at[chip], d2_rs).start()

        return c

    lax.fori_loop(0, 8, owner_send, 0)

    all_of(ya_send, ya_recv, 2).wait_recv()

    def take_a(g, c):
        spread_a(ya_recv[slots_of(g), 0:48], ya_recv[slots_of(g), 48:96], tmp)
        o = nn(up[...], tmp[...]).reshape(L, GR, 256)
        gk[:, rows_of(g), 0:256] = o.astype(BF)
        return c

    lax.fori_loop(0, GROUPS, take_a, 0)

    def out_first(c, carry):
        x = gk[c, :, 0:256]
        r = tn(x, tij[...])
        top = r.astype(BF)
        low = (r - top.astype(F32)).astype(BF)
        cs[c] = nt(x, tijp[:, 0:256]) + (nn(pmt[:, 0:256], top) + nn(pmt[:, 0:256], low))
        pltpu.make_async_copy(cs.at[c], cs_hbm.at[c], ld.at[2]).start()
        return carry

    lax.fori_loop(0, L, out_first, 0)

    is_owner = y == grp

    def fin_copy(ty):
        return pltpu.make_async_remote_copy(
            src_ref=dfin, dst_ref=dfin, send_sem=d3_ss, recv_sem=d3_rs,
            device_id={"vir": v, "trip": ty}, device_id_type=MESH,
        )

    def take_b(s, c):
        g = group_at(s)
        pltpu.make_async_copy(yb_recv.at[slots_of(g)], yb_recv.at[slots_of(g)], yb_rs.at[g]).wait()
        last = spread_b(yb_recv[slots_of(g), 0:48], yb_recv[slots_of(g), 48:80], tmp)
        o = nn(up[...], tmp[...]).reshape(L, GR, 256)
        xb[:, rows_of(g), first] = o.astype(BF)
        xb[L - 1, rows_of(g), rest] = nn(ulast[...], last).astype(BF)
        pltpu.make_async_copy(
            xb.at[:, rows_of(g), first], xo_hbm.at[:, rows_of(g)], ld.at[3]
        ).start()
        pltpu.make_async_copy(
            xb.at[L - 1, rows_of(g), rest], dx_hbm.at[rows_of(g)], ld.at[4]
        ).start()
        return c

    lax.fori_loop(0, 2, take_b, 0)

    @pl.when(is_owner)
    def _():
        pltpu.make_async_copy(d2, d2, d2_rs).wait()
        dfin[...] = jnp.sum(d2[...], axis=0)
        for dy in (1, 2, 3):
            fin_copy(lax.rem(y + dy, 4)).start()

    lax.fori_loop(2, GROUPS, take_b, 0)

    @pl.when(jnp.logical_not(is_owner))
    def _():
        fin_copy(y).wait_recv()

    small[...] = dfin[...] * (1.0 / (V * V))
    sel = iota((1, 128), 1) == y
    es = jnp.sum(jnp.where(sel, dfin[7:8, 0:128], 0.0), axis=1, keepdims=True)
    small[7:8, 0:128] = jnp.broadcast_to(es * (1.0 / V**3), (1, 128))

    out_t.wait()
    out_p.wait()
    pltpu.make_async_copy(cs, cs_hbm, ld.at[2]).wait()
    pltpu.make_async_copy(xb.at[:, :, first], xo_hbm, ld.at[3]).wait()
    pltpu.make_async_copy(xb.at[L - 1, :, rest], dx_hbm, ld.at[4]).wait()
    for h in range(2):
        part = g_send.at[0, pl.ds(0, N - 1)]
        pltpu.make_async_remote_copy(
            src_ref=part, dst_ref=part, send_sem=g_ss.at[h], recv_sem=y_l.at[0],
            device_id={"vir": v, "trip": up_y}, device_id_type=MESH,
        ).wait_send()
        for s in range(GROUPS):
            part = g_send.at[0, pl.ds(0, 2 * GD)]
            pltpu.make_async_remote_copy(
                src_ref=part, dst_ref=part, send_sem=y_ss.at[GROUPS * h + s], recv_sem=y_l.at[0],
                device_id={"vir": v, "trip": up_y}, device_id_type=MESH,
            ).wait_send()
            y_copy(h, y, s, up_y, y_l.at[0], y_fs).wait_send()
    for n, buf in enumerate((sa_send, sb_send, ya_send, yb_send)):
        part = buf.at[pl.ds(0, N - 1)]
        all_of(part, part, n).wait_send()
    part = d1.at[pl.ds(0, 7)]
    pltpu.make_async_remote_copy(
        src_ref=part, dst_ref=part, send_sem=d1_ss, recv_sem=d1_ss,
        device_id={"vir": v, "trip": up_y}, device_id_type=MESH,
    ).wait_send()

    def drain_owner(count):
        q = d2.at[pl.ds(0, count)]
        pltpu.make_async_remote_copy(
            src_ref=q, dst_ref=q, send_sem=d2_ss, recv_sem=d2_ss,
            device_id={"vir": v, "trip": up_y}, device_id_type=MESH,
        ).wait_send()

    own_piece = (v // 8) == piece

    @pl.when(own_piece)
    def _():
        drain_owner(7)

    @pl.when(jnp.logical_not(own_piece))
    def _():
        drain_owner(8)

    @pl.when(is_owner)
    def _():
        for dy in (1, 2, 3):
            fin_copy(lax.rem(y + dy, 4)).wait_send()


def finish(small, cs, xo, dx, tij, tijp, pmt, energy, density, vvvo):
    c = pl.program_id(0)
    x = xo[0, :, 0:192]
    r = tn(x, tij[...]).astype(BF)
    acc = cs[0] + (nt(x, tijp[:, 256:V]) + nn(pmt[:, 256:V], r))

    @pl.when(c < L - 1)
    def _():
        vvvo[0, 0] = acc.astype(BF)

    @pl.when(c == L - 1)
    def _():
        z = dx[...]
        r = tn(z, tij[...]).astype(BF)
        vvvo[0, 0] = (acc + (nt(z, tijp[:, 0:256]) + nn(pmt[:, 0:256], r))).astype(BF)
        density[...] = small[0:7, 0:V]
        energy[0] = jnp.sum(jnp.where(iota((1, 128), 1) == 0, small[7:8, 0:128], 0.0))


def body(triplets, pair_integrals, k_integrals, pair_amplitudes, k_amplitudes, occ_energy, vir_energy):
    vm = pl.BlockSpec(memory_space=pltpu.VMEM)
    sm = pl.BlockSpec(memory_space=pltpu.SMEM)
    hbm = pl.BlockSpec(memory_space=pl.ANY)
    slab = pltpu.VMEM((L, V, V), BF)
    dma = pltpu.SemaphoreType.DMA
    small, cs, xo, dx, tijp, pmt = pl.pallas_call(
        kernel,
        out_shape=(
            jax.ShapeDtypeStruct((8, 512), F32),
            jax.ShapeDtypeStruct((L, V, V), F32),
            jax.ShapeDtypeStruct((L, V, 256), BF),
            jax.ShapeDtypeStruct((V, 256), BF),
            jax.ShapeDtypeStruct((V, V), BF),
            jax.ShapeDtypeStruct((V, V), BF),
        ),
        in_specs=[sm, sm, sm, vm] + [hbm] * 7 + [vm] * 4,
        out_specs=(vm, hbm, hbm, hbm, hbm, hbm),
        scratch_shapes=[
            slab, slab, slab,
            pltpu.VMEM((V, V), BF),
            pltpu.VMEM((1, 2, V, V), BF),
            pltpu.VMEM((GD * SLOT, L * GR), BF),
            pltpu.VMEM((L * GR, GD * SLOT), BF),
            pltpu.VMEM((N * 8, V), BF),
            pltpu.VMEM((L, V, V), F32),
            pltpu.VMEM((L, V, 512), F32),
            pltpu.VMEM((L, V, 512), BF),
        ]
        + [pltpu.VMEM((V, V), BF)] * 6
        + [
            pltpu.VMEM((8, 512), F32),
            pltpu.VMEM((GD * SLOT, 256), BF),
            pltpu.VMEM((GD * 32, 512), BF),
            pltpu.VMEM((2, N, 32, 128), BF),
            pltpu.VMEM((2, 4, N, 32, 128), BF),
            pltpu.VMEM((N, ROWS_A, 128), BF),
            pltpu.VMEM((N, ROWS_A, 128), BF),
            pltpu.VMEM((N, ROWS_B, 128), BF),
            pltpu.VMEM((N, ROWS_B, 128), BF),
            pltpu.VMEM((N, ROWS_A, 128), BF),
            pltpu.VMEM((N, ROWS_A, 128), BF),
            pltpu.VMEM((N, ROWS_B, 128), BF),
            pltpu.VMEM((N, ROWS_B, 128), BF),
            pltpu.VMEM((N * 8, 512), F32),
            pltpu.VMEM((8, 64, 512), F32),
            pltpu.VMEM((32, 8, 512), F32),
            pltpu.VMEM((64, 512), F32),
            pltpu.VMEM((8, 512), F32),
            dma((8,)), dma((2,)), dma((8,)), dma((8,)), dma((8,)), dma((8,)), dma((8,)), dma((8,)),
            dma((4,)), dma((4,)), dma((4,)), dma, dma, dma, dma, dma, dma,
        ],
        compiler_params=pltpu.CompilerParams(
            collective_id=0, has_side_effects=True, vmem_limit_bytes=60 * 1024 * 1024
        ),
        name="triples",
    )(
        triplets, occ_energy, vir_energy, vir_energy.reshape(1, V), pair_integrals, k_integrals,
        pair_amplitudes, k_amplitudes,
        jnp.asarray(pack_matrix(), BF), jnp.asarray(unpack_matrix(), BF), jnp.asarray(row_matrix(), BF),
        jnp.asarray(pack_last(), BF), jnp.asarray(unpack_last(), BF),
        jnp.asarray(turn_pack_matrix(), BF), jnp.asarray(turn_unpack_matrix(), BF),
    )
    whole = lambda shape: pl.BlockSpec(shape, lambda c: (0,) * len(shape))
    return pl.pallas_call(
        finish,
        grid=(L,),
        out_shape=(
            jax.ShapeDtypeStruct((1,), F32),
            jax.ShapeDtypeStruct((L, V), F32),
            jax.ShapeDtypeStruct((1, L, V, V), BF),
        ),
        in_specs=[
            whole((8, 512)),
            pl.BlockSpec((1, V, V), lambda c: (c, 0, 0)),
            pl.BlockSpec((1, V, 256), lambda c: (c, 0, 0)),
            whole((V, 256)),
            whole((V, V)),
            whole((V, V)),
            whole((V, V)),
        ],
        out_specs=(
            pl.BlockSpec(memory_space=pltpu.SMEM),
            whole((L, V)),
            pl.BlockSpec((1, 1, V, V), lambda c: (0, c, 0, 0)),
        ),
        compiler_params=pltpu.CompilerParams(vmem_limit_bytes=60 * 1024 * 1024),
        name="finish",
    )(small, cs, xo, dx, pair_amplitudes, tijp, pmt)


def solution(mesh):
    return jax.shard_map(
        body,
        mesh=mesh,
        in_specs=(
            P("trip", None),
            P(None, "vir", None, None),
            P("trip", "vir", None, None),
            P(),
            P("trip", None, None, None),
            P(),
            P(),
        ),
        out_specs=(P("trip"), P("vir", None), P("trip", "vir", None, None)),
        check_vma=False,
    )
```

```python
import numpy as np
import jax
import jax.numpy as jnp
from jax import lax
from jax.experimental import pallas as pl
from jax.experimental.pallas import tpu as pltpu
from jax.sharding import PartitionSpec as P

MESH = pl.DeviceIdType.MESH
BF, F32 = jnp.bfloat16, jnp.float32
V = 448
N = 64
L = 7
GROUPS = 4
GD = 16
GR = GD * L
SLOT = 64
ROWS_A, ROWS_B = 96, 80


def pack_matrix():
    m = np.zeros((GD, SLOT, L, GD, L), np.float32)
    for p in range(L):
        for q in range(L):
            for j in range(GD):
                m[j, L * p + q, p, j, q] = 1
    return m.reshape(GD * SLOT, L * GR)


def unpack_matrix():
    m = np.zeros((L, GD, L, GD, SLOT), np.float32)
    for p in range(L):
        for q in range(L):
            for k in range(GD):
                m[q, k, p, k, L * p + q] = 1
    return m.reshape(L * GR, GD * SLOT)


def pack_last():
    m = np.zeros((GD, 8, GD, L), np.float32)
    for j in range(GD):
        m[j, :, j, L - 1] = 1
    return m.reshape(GD * 8, GR)


def unpack_last():
    m = np.zeros((GD, L, GD, 8), np.float32)
    for j in range(GD):
        m[j, L - 1, j, 0] = 1
    return m.reshape(GR, GD * 8)


def turn_pack_matrix():
    m = np.zeros((GD, 32, 4, GD, L), np.float32)
    for p in range(4):
        for q in range(L):
            for j in range(GD):
                m[j, L * p + q, p, j, q] = 1
    return m.reshape(GD * 32, 4 * GR)


def turn_unpack_matrix():
    m = np.zeros((L, 4, GD, GD, 32), np.float32)
    for p in range(4):
        for q in range(L):
            for k in range(GD):
                m[q, p, k, k, L * p + q] = 1
    return m.reshape(L * 4 * GD, GD * 32)


def row_matrix():
    m = np.zeros((N, 8, N, L), np.float32)
    for j in range(N):
        for i in range(L):
            m[j, i, j, i] = 1
    return m.reshape(N * 8, V)


def nn(x, y):
    return lax.dot_general(x, y, (((1,), (0,)), ((), ())), preferred_element_type=F32)


def nt(x, y):
    return lax.dot_general(x, y, (((1,), (1,)), ((), ())), preferred_element_type=F32)


def tn(x, y):
    return lax.dot_general(x, y, (((0,), (0,)), ((), ())), preferred_element_type=F32)


def iota(shape, dim):
    return lax.broadcasted_iota(jnp.int32, shape, dim)


def packed_a(x, pk):
    o = nn(pk[...], x).reshape(GD, SLOT, 256)
    return o[:, :48, :128].astype(BF), o[:, :48, 128:].astype(BF)


def packed_b(x, last, pk, pl_ref):
    o = nn(pk[...], x).reshape(GD, SLOT, 256)
    t = nn(pl_ref[...], last).reshape(GD, 8, 256)
    shape = (GD, 32, 128)
    row = iota(shape, 1)
    r0 = jnp.broadcast_to(t[:, 0:1, :128], shape)
    r1 = jnp.broadcast_to(t[:, 0:1, 128:], shape)
    r2 = jnp.broadcast_to(o[:, 48:49, :128], shape)
    high = jnp.where(row == 24, r0, jnp.where(row == 26, r1, jnp.where(row == 30, r2, o[:, 32:64, 128:])))
    high = pltpu.roll(high, 64, 2)
    high = jnp.where(row == 25, r0, jnp.where(row == 27, r1, jnp.where(row == 31, r2, high)))
    mixed = jnp.where(iota(shape, 2) < 64, o[:, :32, 128:], high)
    return o[:, :48, :128].astype(BF), mixed.astype(BF)


def spread_a(m0, m1, tmp):
    zero = jnp.zeros((GD, 16, 128), BF)
    tmp[:, 0:128] = jnp.concatenate([m0, zero], axis=1).reshape(GD * SLOT, 128)
    tmp[:, 128:256] = jnp.concatenate([m1, zero], axis=1).reshape(GD * SLOT, 128)


def spread_b(m0, mixed, tmp):
    mixed = mixed.astype(F32)
    lane = iota((GD, 32, 128), 2) < 64
    turned = pltpu.roll(mixed, 64, 2)
    low = jnp.where(lane, mixed, 0.0).astype(BF)
    high = jnp.where(lane, turned, 0.0).astype(BF)

    def joined(k, rows):
        row = jnp.where(
            iota((GD, 1, 128), 2) < 64, turned[:, k : k + 1, :], mixed[:, k + 1 : k + 2, :]
        )
        return jnp.broadcast_to(row, (GD, rows, 128))

    full = joined(30, 16).astype(BF)
    tmp[:, 0:128] = jnp.concatenate([m0, full], axis=1).reshape(GD * SLOT, 128)
    tmp[:, 128:256] = jnp.concatenate([low, high], axis=1).reshape(GD * SLOT, 128)
    return jnp.concatenate(
        [joined(24, 8).reshape(GD * 8, 128), joined(26, 8).reshape(GD * 8, 128)], axis=1
    ).astype(BF)


def kernel(
    trip_ref, occ_ref, virs_ref, vir_ref, pair_hbm, k_hbm, tij_hbm, kamp_hbm, pk_hbm, up_hbm, row_hbm, plast, ulast, pkt, upt,
    small, cs_hbm, r_hbm, rl_hbm, pmt_hbm,
    gi, gj, gk, tij, kamp, pk, up, rowm, cs, w, xb, tjt, tit, tjp, tijp, pm, pmt, vrow, tmp, tmpt,
    g_send, g_recv, sa_send, sa_recv, sb_send, sb_recv, ya_send, ya_recv, yb_send, yb_recv,
    gram, d1, d2, d2s, dfin,
    ld, g_ss, g_zs, y_ss, y_fs, y_l, y_r, y_o, a_ss, a_rs, yb_rs, d1_ss, d1_rs, d2_ss, d2_rs, d3_ss, d3_rs,
):
    v = lax.axis_index("vir")
    y = lax.axis_index("trip")
    core = lax.rem(v, 2)
    grp = v // GD
    inner = lax.rem(v, GD)
    chip = v // 2

    loads = [
        pltpu.make_async_copy(src, dst, ld.at[n])
        for n, (src, dst) in enumerate(
            (
                (pair_hbm.at[1], gj), (k_hbm.at[0], gk), (tij_hbm, tij), (pk_hbm, pk),
                (pair_hbm.at[0], gi), (kamp_hbm, kamp), (up_hbm, up), (row_hbm, rowm),
            )
        )
    ]
    loads[0].start()

    barrier = pltpu.get_barrier_semaphore()

    def greet(k, c):
        pl.semaphore_signal(
            barrier, inc=1, device_id={"vir": lax.rem(v + k, N), "trip": y}, device_id_type=MESH
        )
        return c

    lax.fori_loop(1, N, greet, 0)
    partner = chip * 2 + (1 - core)
    for dy in (1, 2, 3):
        ty = lax.rem(y + dy, 4)
        pl.semaphore_signal(barrier, inc=1, device_id={"vir": v, "trip": ty}, device_id_type=MESH)
        pl.semaphore_signal(
            barrier, inc=1, device_id={"vir": partner, "trip": ty}, device_id_type=MESH
        )

    loads[0].wait()
    for n in range(1, 8):
        loads[n].start()
    xb[:, :, 384:512] = jnp.zeros((L, V, 128), BF)

    def send_group(src, dst, g, ss, rs):
        def one(k, c):
            d = g * GD + lax.rem(inner + k, GD)

            @pl.when(d != v)
            def _():
                pltpu.make_async_remote_copy(
                    src_ref=src.at[d], dst_ref=dst.at[v], send_sem=ss, recv_sem=rs,
                    device_id={"vir": d, "trip": y}, device_id_type=MESH,
                ).start()

            @pl.when(d == v)
            def _():
                pltpu.make_async_copy(src.at[d], dst.at[v], rs).start()

            return c

        lax.fori_loop(0, GD, one, 0)

    def rows_of(g):
        return pl.ds(pl.multiple_of(g * GR, 16), GR)

    def slots_of(g):
        return pl.ds(g * GD, GD)

    tile = pl.ds(pl.multiple_of(y * 128, 128), 128)

    def turn(s, c):
        g = lax.rem(grp + s, GROUPS)
        xb[:, rows_of(g), 0:V] = gj[:, rows_of(g), :]
        x = xb[0:4, rows_of(g), tile].reshape(4 * GR, 128)
        g_send[0, slots_of(g)] = nn(pkt[...], x).astype(BF).reshape(GD, 32, 128)

        @pl.when(s == 0)
        def _():
            pl.semaphore_wait(barrier, N - 1 + 6)

        send_group(g_send.at[0], g_recv.at[0, y], g, g_ss.at[0], g_zs.at[grp])
        return c

    def turn_rest(s, c):
        g = lax.rem(grp + s, GROUPS)
        x = xb[4:L, rows_of(g), tile].reshape(3 * GR, 128)
        g_send[1, slots_of(g)] = nn(pkt[:, 0 : 3 * GR], x).astype(BF).reshape(GD, 32, 128)
        send_group(g_send.at[1], g_recv.at[1, y], g, g_ss.at[1], g_zs.at[GROUPS + grp])
        return c

    lax.fori_loop(0, GROUPS, turn, 0)
    lax.fori_loop(0, GROUPS, turn_rest, 0)

    up_y, down_y = lax.rem(y + 1, 4), lax.rem(y + 3, 4)
    far_y = lax.rem(y + 2, 4)

    def group_at(s):
        return lax.rem(grp + GROUPS - s, GROUPS)

    def y_copy(h, q, s, ty, rs, ss):
        piece = g_recv.at[h, q, slots_of(group_at(s))]
        return pltpu.make_async_remote_copy(
            src_ref=piece, dst_ref=piece, send_sem=ss.at[GROUPS * h + s],
            recv_sem=rs, device_id={"vir": v, "trip": ty}, device_id_type=MESH,
        )

    def z_step(h, s):
        y_copy(h, y, s, up_y, g_zs.at[GROUPS * h + group_at(s)], y_ss).wait_recv()
        y_copy(h, y, s, up_y, y_l.at[GROUPS * h + s], y_ss).start()
        y_copy(h, y, s, down_y, y_r.at[GROUPS * h + s], y_ss).start()

    def y_step(h, s):
        n = GROUPS * h + s
        y_copy(h, down_y, s, up_y, y_l.at[n], y_ss).wait_recv()
        if s % 2 == 0:
            y_copy(h, down_y, s, up_y, y_o.at[n], y_fs).start()
        y_copy(h, up_y, s, up_y, y_r.at[n], y_ss).wait_recv()
        if s % 2 == 1:
            y_copy(h, up_y, s, down_y, y_o.at[n], y_fs).start()

    def far_step(h, s):
        y_copy(h, far_y, s, up_y, y_o.at[GROUPS * h + s], y_ss).wait_recv()
        g = group_at(s)
        for t in range(4):
            tmpt[:, 128 * t : 128 * t + 128] = g_recv[h, t, slots_of(g)].reshape(GD * 32, 128)
        o = nn(upt[...], tmpt[...]).astype(BF)
        for q in range(L):
            for p in range(4 - h):
                at = pl.ds(pl.multiple_of(64 * (4 * h + p) + GD * g, GD), GD)
                gj[q, at, :] = o[GD * (4 * q + p) : GD * (4 * q + p + 1), 0:V]

    pm[...] = jnp.where(
        iota((V, V), 1) == 7 * (iota((V, V), 0) & 63) + (iota((V, V), 0) >> 6), 1.0, 0.0
    ).astype(BF)
    pmt[...] = jnp.where(
        iota((V, V), 0) == 7 * (iota((V, V), 1) & 63) + (iota((V, V), 1) >> 6), 1.0, 0.0
    ).astype(BF)
    for n in range(1, 3):
        loads[n].wait()
    tijp[...] = nt(tij[...], pm[...]).astype(BF)
    out_p = pltpu.make_async_copy(pmt, pmt_hbm, ld.at[1])
    out_p.start()

    def c_part(c, carry):
        x = gk[c]
        cs[c] = nt(tij[...], nn(pm[...], x).astype(BF)) + nn(x, tijp[...])
        return carry

    def a_part(i, carry):
        x = gi[i]
        w[i, :, 0:V] = nt(x, tjp[...]) + nt(tjt[...], nn(pm[...], x).astype(BF))
        return carry

    lax.fori_loop(0, 3, c_part, 0)
    z_step(0, 0)
    lax.fori_loop(3, 6, c_part, 0)
    z_step(0, 1)
    y_step(0, 0)
    lax.fori_loop(6, L, c_part, 0)
    for n in range(3, 8):
        loads[n].wait()
    z_step(0, 2)
    y_step(0, 1)
    z_step(0, 3)
    y_step(0, 2)
    z_step(1, 0)
    far_step(0, 0)
    y_step(0, 3)
    z_step(1, 1)
    far_step(0, 1)
    far_step(0, 2)
    z_step(1, 2)
    far_step(0, 3)
    z_step(1, 3)
    y_step(1, 0)

    def send_a(src, dst, n):
        def step(s, c):
            g = lax.rem(grp + s, GROUPS)
            m0, m1 = packed_a(xb[:, rows_of(g), 0:256].reshape(L * GR, 256), pk)
            src[slots_of(g), 0:48] = m0
            src[slots_of(g), 48:96] = m1
            send_group(src, dst, g, a_ss.at[n], a_rs.at[n])
            return c

        lax.fori_loop(0, GROUPS, step, 0)

    def send_b(src, dst, n, rs, start, stop):
        def step(s, c):
            g = lax.rem(grp + s, GROUPS)
            x = xb[:, rows_of(g), 256:512].reshape(L * GR, 256)
            m0, mixed = packed_b(x, xb[L - 1, rows_of(g), 0:256], pk, plast)
            src[slots_of(g), 0:48] = m0
            src[slots_of(g), 48:80] = mixed
            send_group(src, dst, g, a_ss.at[n], rs)
            return c

        lax.fori_loop(start, stop, step, 0)

    def all_of(src, dst, n):
        return pltpu.make_async_remote_copy(
            src_ref=src, dst_ref=dst, send_sem=a_ss.at[n], recv_sem=a_rs.at[n],
            device_id={"vir": lax.rem(v + 1, N), "trip": y}, device_id_type=MESH,
        )

    def s_a(c, carry):
        xb[c, :, 0:256] = (cs[c, :, 0:256] + nt(kamp[0, 0], gj[c, 0:256])).astype(BF)
        return carry

    lax.fori_loop(0, L, s_a, 0)
    send_a(sa_send, sa_recv, 0)

    y_step(1, 1)
    tjt[...] = kamp[0, 1].astype(F32).T.astype(BF)
    tit[...] = kamp[0, 0].astype(F32).T.astype(BF)
    tjp[...] = nn(pm[...], kamp[0, 1]).astype(BF)
    vrow[...] = jnp.ones_like(vrow)
    vcol = jnp.sum(
        jnp.where(iota((V, V), 0) == iota((V, V), 1), vir_ref[...], 0.0), axis=1, keepdims=True
    )
    vrow[0:1, 0:V] = jnp.sum(
        jnp.where(iota((V, V), 0) == 7 * (iota((V, V), 1) & 63) + (iota((V, V), 1) >> 6), vcol, 0.0),
        axis=0, keepdims=True,
    )
    y_step(1, 2)
    far_step(1, 0)
    y_step(1, 3)
    far_step(1, 1)
    far_step(1, 2)
    far_step(1, 3)
    w[:, :, 384:512] = jnp.zeros((L, V, 128), F32)

    def s_b(c, carry):
        xb[c, :, 256:V] = (cs[c, :, 256:V] + nt(kamp[0, 0], gj[c, 256:V])).astype(BF)
        return carry

    lax.fori_loop(0, L, s_b, 0)
    send_b(sb_send, sb_recv, 1, a_rs.at[1], 0, GROUPS)

    def b_part(i, carry):
        w[i, :, 0:V] = w[i, :, 0:V] + nt(tit[...], gj[i])
        return carry

    lax.fori_loop(0, L, a_part, 0)
    lax.fori_loop(0, L, b_part, 0)

    shift = occ_ref[trip_ref[0, 0]] + occ_ref[trip_ref[0, 1]] + occ_ref[trip_ref[0, 2]]
    index = iota((V, 1), 0)
    late = (index - 7 * ((index * 9363) >> 16)) == L - 1

    def weigh(i, lanes, mask, e):
        x = w[i, :, lanes]
        den = vcol + (vrow[0:1, lanes] + (virs_ref[v * L + i] - shift))
        z = x / den
        xb[i, :, lanes] = z.astype(BF)
        t = x * z
        if mask is not None:
            t = jnp.where(mask, t, 0.0)
        return e + jnp.sum(t, axis=0, keepdims=True)

    first, rest = slice(0, 256), slice(256, 512)
    all_of(sa_send, sa_recv, 0).wait_recv()

    def add_a(g, c):
        spread_a(sa_recv[slots_of(g), 0:48], sa_recv[slots_of(g), 48:96], tmp)
        o = nn(up[...], tmp[...]).reshape(L, GR, 256)
        w[:, rows_of(g), first] = w[:, rows_of(g), first] + o
        return c

    lax.fori_loop(0, GROUPS, add_a, 0)
    e = jnp.zeros((1, 256), F32)
    e = lax.fori_loop(0, L - 1, lambda i, e: weigh(i, first, None, e), e)
    e = weigh(L - 1, first, jnp.logical_not(late), e)
    send_a(ya_send, ya_recv, 2)

    def gram_a(i, acc):
        x = xb[i, :, first]
        return acc + nt(x, x)

    cs[0] = lax.fori_loop(0, L - 1, gram_a, jnp.zeros((V, V), F32))

    all_of(sb_send, sb_recv, 1).wait_recv()

    def add_b(g, c):
        last = spread_b(sb_recv[slots_of(g), 0:48], sb_recv[slots_of(g), 48:80], tmp)
        o = nn(up[...], tmp[...]).reshape(L, GR, 256)
        w[:, rows_of(g), rest] = w[:, rows_of(g), rest] + o
        w[L - 1, rows_of(g), first] = w[L - 1, rows_of(g), first] + nn(ulast[...], last)
        return c

    lax.fori_loop(0, GROUPS, add_b, 0)
    e = lax.fori_loop(0, L, lambda i, e: weigh(i, rest, None, e), e)
    e = weigh(L - 1, first, late, e)

    def gram_b(i, acc):
        x = xb[i, :, rest]
        return acc + nt(x, x)

    x = xb[L - 1, :, first]
    total = lax.fori_loop(0, L, gram_b, cs[0] + nt(x, x))

    hi = total.astype(BF)
    left = total - hi.astype(F32)
    mid = left.astype(BF)
    lo = (left - mid.astype(F32)).astype(BF)
    rows = nn(rowm[...], hi) + nn(rowm[...], mid) + nn(rowm[...], lo)
    energy = jnp.sum(e)
    gram[:, 384:512] = jnp.zeros((N * 8, 128), F32)
    gram[:, 0:V] = rows
    spare = lax.rem(iota((N * 8, 128), 0), 8) == 7
    mine = spare & (iota((N * 8, 128), 1) == y)
    gram[:, 0:128] = jnp.where(mine, energy, gram[:, 0:128])

    piece = y * 2 + core

    def piece_copy(k):
        to = lax.rem(piece + k, 8)
        return pltpu.make_async_remote_copy(
            src_ref=gram.at[pl.ds(pl.multiple_of(to * 64, 64), 64)], dst_ref=d1.at[piece],
            send_sem=d1_ss, recv_sem=d1_rs,
            device_id={"vir": chip * 2 + lax.rem(to, 2), "trip": to // 2}, device_id_type=MESH,
        )

    for k in range(1, 8):
        piece_copy(k).start()
    pltpu.make_async_copy(
        gram.at[pl.ds(pl.multiple_of(piece * 64, 64), 64)], d1.at[piece], d1_rs
    ).start()

    send_b(yb_send, yb_recv, 3, yb_rs.at[grp], 0, 2)

    pltpu.make_async_copy(d1, d1, d1_rs).wait()
    d2s[...] = jnp.sum(d1[...], axis=0)

    def owner_send(o, c):
        to = piece * 8 + o
        src = d2s.at[pl.ds(pl.multiple_of(o * 8, 8), 8)]

        @pl.when(to != v)
        def _():
            pltpu.make_async_remote_copy(
                src_ref=src, dst_ref=d2.at[chip], send_sem=d2_ss, recv_sem=d2_rs,
                device_id={"vir": to, "trip": y}, device_id_type=MESH,
            ).start()

        @pl.when(to == v)
        def _():
            pltpu.make_async_copy(src, d2.at[chip], d2_rs).start()

        return c

    lax.fori_loop(0, 8, owner_send, 0)

    send_b(yb_send, yb_recv, 3, yb_rs.at[grp], 2, GROUPS)

    all_of(ya_send, ya_recv, 2).wait_recv()

    def take_a(g, c):
        spread_a(ya_recv[slots_of(g), 0:48], ya_recv[slots_of(g), 48:96], tmp)
        o = nn(up[...], tmp[...]).reshape(L, GR, 256)
        gk[:, rows_of(g), 0:256] = o.astype(BF)
        return c

    lax.fori_loop(0, GROUPS, take_a, 0)

    def out_first(c, carry):
        x = gk[c, :, 0:256]
        r = tn(x, tij[...])
        top = r.astype(BF)
        low = (r - top.astype(F32)).astype(BF)
        cs[c] = nt(x, tijp[:, 0:256]) + (nn(pmt[:, 0:256], top) + nn(pmt[:, 0:256], low))
        return carry

    lax.fori_loop(0, L, out_first, 0)

    is_owner = y == grp

    def fin_copy(ty):
        return pltpu.make_async_remote_copy(
            src_ref=dfin, dst_ref=dfin, send_sem=d3_ss, recv_sem=d3_rs,
            device_id={"vir": v, "trip": ty}, device_id_type=MESH,
        )

    def take_b(s, c):
        g = group_at(s)
        pltpu.make_async_copy(yb_recv.at[slots_of(g)], yb_recv.at[slots_of(g)], yb_rs.at[g]).wait()
        last = spread_b(yb_recv[slots_of(g), 0:48], yb_recv[slots_of(g), 48:80], tmp)
        o = nn(up[...], tmp[...]).astype(BF)[:, 0:192]
        t = tij[rows_of(g), :]
        m = nt(o, tijp[:, 256:V]).reshape(L, GR, V)
        cs[:, rows_of(g), :] = cs[:, rows_of(g), :] + m
        for i in range(L):
            w[i, 0:192, 0:V] = w[i, 0:192, 0:V] + tn(o[GR * i : GR * (i + 1)], t)
        z = nn(ulast[...], last).astype(BF)
        cs[L - 1, rows_of(g), :] = cs[L - 1, rows_of(g), :] + nt(z, tijp[:, 0:256])
        w[0, 192:V, 0:V] = w[0, 192:V, 0:V] + tn(z, t)
        pltpu.make_async_copy(
            cs.at[:, rows_of(g)], cs_hbm.at[:, rows_of(g)], ld.at[2]
        ).start()
        return c

    w[:, 0:192, :] = jnp.zeros((L, 192, 512), F32)
    w[0, 192:V, :] = jnp.zeros((256, 512), F32)
    lax.fori_loop(0, 1, take_b, 0)

    @pl.when(is_owner)
    def _():
        pltpu.make_async_copy(d2, d2, d2_rs).wait()
        dfin[...] = jnp.sum(d2[...], axis=0)
        for dy in (1, 2, 3):
            fin_copy(lax.rem(y + dy, 4)).start()

    lax.fori_loop(1, GROUPS, take_b, 0)
    gi[:, 0:192, :] = w[:, 0:192, 0:V].astype(BF)
    gk[0, 0:256, :] = w[0, 192:V, 0:V].astype(BF)
    out_r = pltpu.make_async_copy(gi.at[:, pl.ds(0, 192)], r_hbm, ld.at[3])
    out_l = pltpu.make_async_copy(gk.at[0, pl.ds(0, 256)], rl_hbm, ld.at[4])
    out_r.start()
    out_l.start()

    @pl.when(jnp.logical_not(is_owner))
    def _():
        fin_copy(y).wait_recv()

    small[...] = dfin[...] * (1.0 / (V * V))
    sel = iota((1, 128), 1) == y
    es = jnp.sum(jnp.where(sel, dfin[7:8, 0:128], 0.0), axis=1, keepdims=True)
    small[7:8, 0:128] = jnp.broadcast_to(es * (1.0 / V**3), (1, 128))

    out_p.wait()
    pltpu.make_async_copy(cs, cs_hbm, ld.at[2]).wait()
    out_r.wait()
    out_l.wait()
    for h in range(2):
        part = g_send.at[0, pl.ds(0, N - 1)]
        pltpu.make_async_remote_copy(
            src_ref=part, dst_ref=part, send_sem=g_ss.at[h], recv_sem=y_l.at[0],
            device_id={"vir": v, "trip": up_y}, device_id_type=MESH,
        ).wait_send()
        for s in range(GROUPS):
            part = g_send.at[0, pl.ds(0, 2 * GD)]
            pltpu.make_async_remote_copy(
                src_ref=part, dst_ref=part, send_sem=y_ss.at[GROUPS * h + s], recv_sem=y_l.at[0],
                device_id={"vir": v, "trip": up_y}, device_id_type=MESH,
            ).wait_send()
            y_copy(h, y, s, up_y, y_l.at[0], y_fs).wait_send()
    for n, buf in enumerate((sa_send, sb_send, ya_send, yb_send)):
        part = buf.at[pl.ds(0, N - 1)]
        all_of(part, part, n).wait_send()
    part = d1.at[pl.ds(0, 7)]
    pltpu.make_async_remote_copy(
        src_ref=part, dst_ref=part, send_sem=d1_ss, recv_sem=d1_ss,
        device_id={"vir": v, "trip": up_y}, device_id_type=MESH,
    ).wait_send()

    def drain_owner(count):
        q = d2.at[pl.ds(0, count)]
        pltpu.make_async_remote_copy(
            src_ref=q, dst_ref=q, send_sem=d2_ss, recv_sem=d2_ss,
            device_id={"vir": v, "trip": up_y}, device_id_type=MESH,
        ).wait_send()

    own_piece = (v // 8) == piece

    @pl.when(own_piece)
    def _():
        drain_owner(7)

    @pl.when(jnp.logical_not(own_piece))
    def _():
        drain_owner(8)

    @pl.when(is_owner)
    def _():
        for dy in (1, 2, 3):
            fin_copy(lax.rem(y + dy, 4)).wait_send()


def finish(small, cs, r, rl, pmt, energy, density, vvvo):
    c = pl.program_id(0)
    acc = cs[0] + nn(pmt[:, 256:V], r[0])

    @pl.when(c < L - 1)
    def _():
        vvvo[0, 0] = acc.astype(BF)

    @pl.when(c == L - 1)
    def _():
        vvvo[0, 0] = (acc + nn(pmt[:, 0:256], rl[...])).astype(BF)
        density[...] = small[0:7, 0:V]
        energy[0] = jnp.sum(jnp.where(iota((1, 128), 1) == 0, small[7:8, 0:128], 0.0))


def body(triplets, pair_integrals, k_integrals, pair_amplitudes, k_amplitudes, occ_energy, vir_energy):
    vm = pl.BlockSpec(memory_space=pltpu.VMEM)
    sm = pl.BlockSpec(memory_space=pltpu.SMEM)
    hbm = pl.BlockSpec(memory_space=pl.ANY)
    slab = pltpu.VMEM((L, V, V), BF)
    dma = pltpu.SemaphoreType.DMA
    small, cs, r, rl, pmt = pl.pallas_call(
        kernel,
        out_shape=(
            jax.ShapeDtypeStruct((8, 512), F32),
            jax.ShapeDtypeStruct((L, V, V), F32),
            jax.ShapeDtypeStruct((L, 192, V), BF),
            jax.ShapeDtypeStruct((256, V), BF),
            jax.ShapeDtypeStruct((V, V), BF),
        ),
        in_specs=[sm, sm, sm, vm] + [hbm] * 7 + [vm] * 4,
        out_specs=(vm, hbm, hbm, hbm, hbm),
        scratch_shapes=[
            slab, slab, slab,
            pltpu.VMEM((V, V), BF),
            pltpu.VMEM((1, 2, V, V), BF),
            pltpu.VMEM((GD * SLOT, L * GR), BF),
            pltpu.VMEM((L * GR, GD * SLOT), BF),
            pltpu.VMEM((N * 8, V), BF),
            pltpu.VMEM((L, V, V), F32),
            pltpu.VMEM((L, V, 512), F32),
            pltpu.VMEM((L, V, 512), BF),
        ]
        + [pltpu.VMEM((V, V), BF)] * 6
        + [
            pltpu.VMEM((8, 512), F32),
            pltpu.VMEM((GD * SLOT, 256), BF),
            pltpu.VMEM((GD * 32, 512), BF),
            pltpu.VMEM((2, N, 32, 128), BF),
            pltpu.VMEM((2, 4, N, 32, 128), BF),
            pltpu.VMEM((N, ROWS_A, 128), BF),
            pltpu.VMEM((N, ROWS_A, 128), BF),
            pltpu.VMEM((N, ROWS_B, 128), BF),
            pltpu.VMEM((N, ROWS_B, 128), BF),
            pltpu.VMEM((N, ROWS_A, 128), BF),
            pltpu.VMEM((N, ROWS_A, 128), BF),
            pltpu.VMEM((N, ROWS_B, 128), BF),
            pltpu.VMEM((N, ROWS_B, 128), BF),
            pltpu.VMEM((N * 8, 512), F32),
            pltpu.VMEM((8, 64, 512), F32),
            pltpu.VMEM((32, 8, 512), F32),
            pltpu.VMEM((64, 512), F32),
            pltpu.VMEM((8, 512), F32),
            dma((8,)), dma((2,)), dma((8,)), dma((8,)), dma((8,)), dma((8,)), dma((8,)), dma((8,)),
            dma((4,)), dma((4,)), dma((4,)), dma, dma, dma, dma, dma, dma,
        ],
        compiler_params=pltpu.CompilerParams(
            collective_id=0, has_side_effects=True, vmem_limit_bytes=60 * 1024 * 1024
        ),
        name="triples",
    )(
        triplets, occ_energy, vir_energy, vir_energy.reshape(1, V), pair_integrals, k_integrals,
        pair_amplitudes, k_amplitudes,
        jnp.asarray(pack_matrix(), BF), jnp.asarray(unpack_matrix(), BF), jnp.asarray(row_matrix(), BF),
        jnp.asarray(pack_last(), BF), jnp.asarray(unpack_last(), BF),
        jnp.asarray(turn_pack_matrix(), BF), jnp.asarray(turn_unpack_matrix(), BF),
    )
    whole = lambda shape: pl.BlockSpec(shape, lambda c: (0,) * len(shape))
    return pl.pallas_call(
        finish,
        grid=(L,),
        out_shape=(
            jax.ShapeDtypeStruct((1,), F32),
            jax.ShapeDtypeStruct((L, V), F32),
            jax.ShapeDtypeStruct((1, L, V, V), BF),
        ),
        in_specs=[
            whole((8, 512)),
            pl.BlockSpec((1, V, V), lambda c: (c, 0, 0)),
            pl.BlockSpec((1, 192, V), lambda c: (c, 0, 0)),
            whole((256, V)),
            whole((V, V)),
        ],
        out_specs=(
            pl.BlockSpec(memory_space=pltpu.SMEM),
            whole((L, V)),
            pl.BlockSpec((1, 1, V, V), lambda c: (0, c, 0, 0)),
        ),
        compiler_params=pltpu.CompilerParams(vmem_limit_bytes=60 * 1024 * 1024),
        name="finish",
    )(small, cs, r, rl, pmt)


def solution(mesh):
    return jax.shard_map(
        body,
        mesh=mesh,
        in_specs=(
            P("trip", None),
            P(None, "vir", None, None),
            P("trip", "vir", None, None),
            P(),
            P("trip", None, None, None),
            P(),
            P(),
        ),
        out_specs=(P("trip"), P("vir", None), P("trip", "vir", None, None)),
        check_vma=False,
    )
```

```python
import numpy as np
import jax
import jax.numpy as jnp
from jax import lax
from jax.experimental import pallas as pl
from jax.experimental.pallas import tpu as pltpu
from jax.sharding import PartitionSpec as P

MESH = pl.DeviceIdType.MESH
BF, F32 = jnp.bfloat16, jnp.float32
V = 448
N = 64
L = 7
GROUPS = 4
GD = 16
GR = GD * L
SLOT = 64
ROWS_A, ROWS_B = 96, 80


def pack_matrix():
    m = np.zeros((GD, SLOT, L, GD, L), np.float32)
    for p in range(L):
        for q in range(L):
            for j in range(GD):
                m[j, L * p + q, p, j, q] = 1
    return m.reshape(GD * SLOT, L * GR)


def unpack_matrix():
    m = np.zeros((L, GD, L, GD, SLOT), np.float32)
    for p in range(L):
        for q in range(L):
            for k in range(GD):
                m[q, k, p, k, L * p + q] = 1
    return m.reshape(L * GR, GD * SLOT)


def pack_last():
    m = np.zeros((GD, 8, GD, L), np.float32)
    for j in range(GD):
        m[j, :, j, L - 1] = 1
    return m.reshape(GD * 8, GR)


def unpack_last():
    m = np.zeros((GD, L, GD, 8), np.float32)
    for j in range(GD):
        m[j, L - 1, j, 0] = 1
    return m.reshape(GR, GD * 8)


def turn_pack_matrix():
    m = np.zeros((GD, 32, 4, GD, L), np.float32)
    for p in range(4):
        for q in range(L):
            for j in range(GD):
                m[j, L * p + q, p, j, q] = 1
    return m.reshape(GD * 32, 4 * GR)


def turn_unpack_matrix():
    m = np.zeros((L, 4, GD, GD, 32), np.float32)
    for p in range(4):
        for q in range(L):
            for k in range(GD):
                m[q, p, k, k, L * p + q] = 1
    return m.reshape(L * 4 * GD, GD * 32)


def row_matrix():
    m = np.zeros((N, 8, N, L), np.float32)
    for j in range(N):
        for i in range(L):
            m[j, i, j, i] = 1
    return m.reshape(N * 8, V)


def nn(x, y):
    return lax.dot_general(x, y, (((1,), (0,)), ((), ())), preferred_element_type=F32)


def nt(x, y):
    return lax.dot_general(x, y, (((1,), (1,)), ((), ())), preferred_element_type=F32)


def tn(x, y):
    return lax.dot_general(x, y, (((0,), (0,)), ((), ())), preferred_element_type=F32)


def iota(shape, dim):
    return lax.broadcasted_iota(jnp.int32, shape, dim)


def packed_a(x, pk):
    o = nn(pk[...], x).reshape(GD, SLOT, 256)
    return o[:, :48, :128].astype(BF), o[:, :48, 128:].astype(BF)


def packed_b(x, last, pk, pl_ref):
    o = nn(pk[...], x).reshape(GD, SLOT, 256)
    t = nn(pl_ref[...], last).reshape(GD, 8, 256)
    shape = (GD, 32, 128)
    row = iota(shape, 1)
    r0 = jnp.broadcast_to(t[:, 0:1, :128], shape)
    r1 = jnp.broadcast_to(t[:, 0:1, 128:], shape)
    r2 = jnp.broadcast_to(o[:, 48:49, :128], shape)
    high = jnp.where(row == 24, r0, jnp.where(row == 26, r1, jnp.where(row == 30, r2, o[:, 32:64, 128:])))
    high = pltpu.roll(high, 64, 2)
    high = jnp.where(row == 25, r0, jnp.where(row == 27, r1, jnp.where(row == 31, r2, high)))
    mixed = jnp.where(iota(shape, 2) < 64, o[:, :32, 128:], high)
    return o[:, :48, :128].astype(BF), mixed.astype(BF)


def spread_a(m0, m1, tmp):
    zero = jnp.zeros((GD, 16, 128), BF)
    tmp[:, 0:128] = jnp.concatenate([m0, zero], axis=1).reshape(GD * SLOT, 128)
    tmp[:, 128:256] = jnp.concatenate([m1, zero], axis=1).reshape(GD * SLOT, 128)


def spread_b(m0, mixed, tmp):
    mixed = mixed.astype(F32)
    lane = iota((GD, 32, 128), 2) < 64
    turned = pltpu.roll(mixed, 64, 2)
    low = jnp.where(lane, mixed, 0.0).astype(BF)
    high = jnp.where(lane, turned, 0.0).astype(BF)

    def joined(k, rows):
        row = jnp.where(
            iota((GD, 1, 128), 2) < 64, turned[:, k : k + 1, :], mixed[:, k + 1 : k + 2, :]
        )
        return jnp.broadcast_to(row, (GD, rows, 128))

    full = joined(30, 16).astype(BF)
    tmp[:, 0:128] = jnp.concatenate([m0, full], axis=1).reshape(GD * SLOT, 128)
    tmp[:, 128:256] = jnp.concatenate([low, high], axis=1).reshape(GD * SLOT, 128)
    return jnp.concatenate(
        [joined(24, 8).reshape(GD * 8, 128), joined(26, 8).reshape(GD * 8, 128)], axis=1
    ).astype(BF)


def kernel(
    trip_ref, occ_ref, virs_ref, vir_ref, pair_hbm, k_hbm, tij_hbm, kamp_hbm, pk_hbm, up_hbm, row_hbm, plast, ulast, pkt, upt,
    small, cs_hbm, r_hbm, rl_hbm, pmt_hbm,
    gi, gj, gk, tij, kamp, pk, up, rowm, cs, w, xb, tjt, tit, tjp, tijp, pm, pmt, vrow, tmp, tmpt,
    g_send, g_recv, sa_send, sa_recv, sb_send, sb_recv, ya_send, ya_recv, yb_send, yb_recv,
    gram, d1, d2, d2s, dfin,
    ld, g_ss, g_zs, y_ss, y_fs, y_l, y_r, y_o, a_ss, a_rs, yb_rs, d1_ss, d1_rs, d2_ss, d2_rs, d3_ss, d3_rs,
):
    v = lax.axis_index("vir")
    y = lax.axis_index("trip")
    core = lax.rem(v, 2)
    grp = v // GD
    inner = lax.rem(v, GD)
    chip = v // 2

    loads = [
        pltpu.make_async_copy(src, dst, ld.at[n])
        for n, (src, dst) in enumerate(
            (
                (pair_hbm.at[1], gj), (k_hbm.at[0], gk), (tij_hbm, tij), (pk_hbm, pk),
                (pair_hbm.at[0], gi), (kamp_hbm, kamp), (up_hbm, up), (row_hbm, rowm),
            )
        )
    ]
    loads[0].start()

    barrier = pltpu.get_barrier_semaphore()

    def greet(k, c):
        pl.semaphore_signal(
            barrier, inc=1, device_id={"vir": lax.rem(v + k, N), "trip": y}, device_id_type=MESH
        )
        return c

    lax.fori_loop(1, N, greet, 0)
    partner = chip * 2 + (1 - core)
    for dy in (1, 2, 3):
        ty = lax.rem(y + dy, 4)
        pl.semaphore_signal(barrier, inc=1, device_id={"vir": v, "trip": ty}, device_id_type=MESH)
        pl.semaphore_signal(
            barrier, inc=1, device_id={"vir": partner, "trip": ty}, device_id_type=MESH
        )

    loads[0].wait()
    for n in range(1, 8):
        loads[n].start()
    xb[:, :, 384:512] = jnp.zeros((L, V, 128), BF)

    def send_group(src, dst, g, ss, rs):
        def one(k, c):
            d = g * GD + lax.rem(inner + k, GD)

            @pl.when(d != v)
            def _():
                pltpu.make_async_remote_copy(
                    src_ref=src.at[d], dst_ref=dst.at[v], send_sem=ss, recv_sem=rs,
                    device_id={"vir": d, "trip": y}, device_id_type=MESH,
                ).start()

            @pl.when(d == v)
            def _():
                pltpu.make_async_copy(src.at[d], dst.at[v], rs).start()

            return c

        lax.fori_loop(0, GD, one, 0)

    def rows_of(g):
        return pl.ds(pl.multiple_of(g * GR, 16), GR)

    def slots_of(g):
        return pl.ds(g * GD, GD)

    tile = pl.ds(pl.multiple_of(y * 128, 128), 128)

    def turn(s, c):
        g = lax.rem(grp + s, GROUPS)
        xb[:, rows_of(g), 0:V] = gj[:, rows_of(g), :]
        x = xb[0:4, rows_of(g), tile].reshape(4 * GR, 128)
        g_send[0, slots_of(g)] = nn(pkt[...], x).astype(BF).reshape(GD, 32, 128)

        @pl.when(s == 0)
        def _():
            pl.semaphore_wait(barrier, N - 1 + 6)

        send_group(g_send.at[0], g_recv.at[0, y], g, g_ss.at[0], g_zs.at[grp])
        return c

    def turn_rest(s, c):
        g = lax.rem(grp + s, GROUPS)
        x = xb[4:L, rows_of(g), tile].reshape(3 * GR, 128)
        g_send[1, slots_of(g)] = nn(pkt[:, 0 : 3 * GR], x).astype(BF).reshape(GD, 32, 128)
        send_group(g_send.at[1], g_recv.at[1, y], g, g_ss.at[1], g_zs.at[GROUPS + grp])
        return c

    lax.fori_loop(0, GROUPS, turn, 0)
    lax.fori_loop(0, GROUPS, turn_rest, 0)

    up_y, down_y = lax.rem(y + 1, 4), lax.rem(y + 3, 4)
    far_y = lax.rem(y + 2, 4)

    def group_at(s):
        return lax.rem(grp + GROUPS - s, GROUPS)

    def y_copy(h, q, s, ty, rs, ss):
        piece = g_recv.at[h, q, slots_of(group_at(s))]
        return pltpu.make_async_remote_copy(
            src_ref=piece, dst_ref=piece, send_sem=ss.at[GROUPS * h + s],
            recv_sem=rs, device_id={"vir": v, "trip": ty}, device_id_type=MESH,
        )

    def z_step(h, s):
        y_copy(h, y, s, up_y, g_zs.at[GROUPS * h + group_at(s)], y_ss).wait_recv()
        y_copy(h, y, s, up_y, y_l.at[GROUPS * h + s], y_ss).start()
        y_copy(h, y, s, down_y, y_r.at[GROUPS * h + s], y_ss).start()

    def y_step(h, s):
        n = GROUPS * h + s
        y_copy(h, down_y, s, up_y, y_l.at[n], y_ss).wait_recv()
        if s % 2 == 0:
            y_copy(h, down_y, s, up_y, y_o.at[n], y_fs).start()
        y_copy(h, up_y, s, up_y, y_r.at[n], y_ss).wait_recv()
        if s % 2 == 1:
            y_copy(h, up_y, s, down_y, y_o.at[n], y_fs).start()

    def far_step(h, s):
        y_copy(h, far_y, s, up_y, y_o.at[GROUPS * h + s], y_ss).wait_recv()
        g = group_at(s)
        for t in range(4):
            tmpt[:, 128 * t : 128 * t + 128] = g_recv[h, t, slots_of(g)].reshape(GD * 32, 128)
        o = nn(upt[...], tmpt[...]).astype(BF)
        for q in range(L):
            for p in range(4 - h):
                at = pl.ds(pl.multiple_of(64 * (4 * h + p) + GD * g, GD), GD)
                gj[q, at, :] = o[GD * (4 * q + p) : GD * (4 * q + p + 1), 0:V]

    z_step(0, 0)

    pm[...] = jnp.where(
        iota((V, V), 1) == 7 * (iota((V, V), 0) & 63) + (iota((V, V), 0) >> 6), 1.0, 0.0
    ).astype(BF)
    pmt[...] = jnp.where(
        iota((V, V), 0) == 7 * (iota((V, V), 1) & 63) + (iota((V, V), 1) >> 6), 1.0, 0.0
    ).astype(BF)
    for n in range(1, 3):
        loads[n].wait()
    tijp[...] = nt(tij[...], pm[...]).astype(BF)
    out_p = pltpu.make_async_copy(pmt, pmt_hbm, ld.at[1])
    out_p.start()

    def c_part(c, carry):
        x = gk[c]
        cs[c] = nt(tij[...], nn(pm[...], x).astype(BF)) + nn(x, tijp[...])
        return carry

    def a_part(i, carry):
        x = gi[i]
        w[i, :, 0:V] = nt(x, tjp[...]) + nt(tjt[...], nn(pm[...], x).astype(BF))
        return carry

    z_step(0, 1)
    lax.fori_loop(0, 1, c_part, 0)
    z_step(0, 2)
    y_step(0, 0)
    lax.fori_loop(1, 3, c_part, 0)
    z_step(0, 3)
    y_step(0, 1)
    lax.fori_loop(3, 5, c_part, 0)
    y_step(0, 2)
    for n in range(3, 8):
        loads[n].wait()
    far_step(0, 0)
    lax.fori_loop(5, L, c_part, 0)
    y_step(0, 3)
    z_step(1, 0)
    far_step(0, 1)
    z_step(1, 1)
    far_step(0, 2)
    far_step(0, 3)

    def send_a(src, dst, n):
        def step(s, c):
            g = lax.rem(grp + s, GROUPS)
            m0, m1 = packed_a(xb[:, rows_of(g), 0:256].reshape(L * GR, 256), pk)
            src[slots_of(g), 0:48] = m0
            src[slots_of(g), 48:96] = m1
            send_group(src, dst, g, a_ss.at[n], a_rs.at[n])
            return c

        lax.fori_loop(0, GROUPS, step, 0)

    def send_b(src, dst, n, rs, start, stop):
        def step(s, c):
            g = lax.rem(grp + s, GROUPS)
            x = xb[:, rows_of(g), 256:512].reshape(L * GR, 256)
            m0, mixed = packed_b(x, xb[L - 1, rows_of(g), 0:256], pk, plast)
            src[slots_of(g), 0:48] = m0
            src[slots_of(g), 48:80] = mixed
            send_group(src, dst, g, a_ss.at[n], rs)
            return c

        lax.fori_loop(start, stop, step, 0)

    def all_of(src, dst, n):
        return pltpu.make_async_remote_copy(
            src_ref=src, dst_ref=dst, send_sem=a_ss.at[n], recv_sem=a_rs.at[n],
            device_id={"vir": lax.rem(v + 1, N), "trip": y}, device_id_type=MESH,
        )

    def s_a(c, carry):
        xb[c, :, 0:256] = (cs[c, :, 0:256] + nt(kamp[0, 0], gj[c, 0:256])).astype(BF)
        return carry

    lax.fori_loop(0, L, s_a, 0)
    z_step(1, 2)
    send_a(sa_send, sa_recv, 0)

    z_step(1, 3)
    y_step(1, 0)
    y_step(1, 1)
    tjt[...] = kamp[0, 1].astype(F32).T.astype(BF)
    tit[...] = kamp[0, 0].astype(F32).T.astype(BF)
    tjp[...] = nn(pm[...], kamp[0, 1]).astype(BF)
    vrow[...] = jnp.ones_like(vrow)
    vcol = jnp.sum(
        jnp.where(iota((V, V), 0) == iota((V, V), 1), vir_ref[...], 0.0), axis=1, keepdims=True
    )
    vrow[0:1, 0:V] = jnp.sum(
        jnp.where(iota((V, V), 0) == 7 * (iota((V, V), 1) & 63) + (iota((V, V), 1) >> 6), vcol, 0.0),
        axis=0, keepdims=True,
    )
    y_step(1, 2)
    far_step(1, 0)
    y_step(1, 3)
    far_step(1, 1)
    far_step(1, 2)
    far_step(1, 3)
    w[:, :, 384:512] = jnp.zeros((L, V, 128), F32)

    def s_b(c, carry):
        xb[c, :, 256:V] = (cs[c, :, 256:V] + nt(kamp[0, 0], gj[c, 256:V])).astype(BF)
        return carry

    lax.fori_loop(0, L, s_b, 0)
    send_b(sb_send, sb_recv, 1, a_rs.at[1], 0, GROUPS)

    def b_part(i, carry):
        w[i, :, 0:V] = w[i, :, 0:V] + nt(tit[...], gj[i])
        return carry

    lax.fori_loop(0, L, a_part, 0)
    lax.fori_loop(0, L, b_part, 0)

    shift = occ_ref[trip_ref[0, 0]] + occ_ref[trip_ref[0, 1]] + occ_ref[trip_ref[0, 2]]
    index = iota((V, 1), 0)
    late = (index - 7 * ((index * 9363) >> 16)) == L - 1

    def weigh(i, lanes, mask, e):
        x = w[i, :, lanes]
        den = vcol + (vrow[0:1, lanes] + (virs_ref[v * L + i] - shift))
        z = x / den
        xb[i, :, lanes] = z.astype(BF)
        t = x * z
        if mask is not None:
            t = jnp.where(mask, t, 0.0)
        return e + jnp.sum(t, axis=0, keepdims=True)

    first, rest = slice(0, 256), slice(256, 512)
    all_of(sa_send, sa_recv, 0).wait_recv()

    def add_a(g, c):
        spread_a(sa_recv[slots_of(g), 0:48], sa_recv[slots_of(g), 48:96], tmp)
        o = nn(up[...], tmp[...]).reshape(L, GR, 256)
        w[:, rows_of(g), first] = w[:, rows_of(g), first] + o
        return c

    lax.fori_loop(0, GROUPS, add_a, 0)
    e = jnp.zeros((1, 256), F32)
    e = lax.fori_loop(0, L - 1, lambda i, e: weigh(i, first, None, e), e)
    e = weigh(L - 1, first, jnp.logical_not(late), e)
    send_a(ya_send, ya_recv, 2)

    def gram_a(i, acc):
        x = xb[i, :, first]
        return acc + nt(x, x)

    cs[0] = lax.fori_loop(0, L - 1, gram_a, jnp.zeros((V, V), F32))

    all_of(sb_send, sb_recv, 1).wait_recv()

    def add_b(g, c):
        last = spread_b(sb_recv[slots_of(g), 0:48], sb_recv[slots_of(g), 48:80], tmp)
        o = nn(up[...], tmp[...]).reshape(L, GR, 256)
        w[:, rows_of(g), rest] = w[:, rows_of(g), rest] + o
        w[L - 1, rows_of(g), first] = w[L - 1, rows_of(g), first] + nn(ulast[...], last)
        return c

    lax.fori_loop(0, GROUPS, add_b, 0)
    e = lax.fori_loop(0, L, lambda i, e: weigh(i, rest, None, e), e)
    e = weigh(L - 1, first, late, e)

    def gram_b(i, acc):
        x = xb[i, :, rest]
        return acc + nt(x, x)

    x = xb[L - 1, :, first]
    total = lax.fori_loop(0, L, gram_b, cs[0] + nt(x, x))

    hi = total.astype(BF)
    left = total - hi.astype(F32)
    mid = left.astype(BF)
    lo = (left - mid.astype(F32)).astype(BF)
    rows = nn(rowm[...], hi) + nn(rowm[...], mid) + nn(rowm[...], lo)
    energy = jnp.sum(e)
    gram[:, 384:512] = jnp.zeros((N * 8, 128), F32)
    gram[:, 0:V] = rows
    spare = lax.rem(iota((N * 8, 128), 0), 8) == 7
    mine = spare & (iota((N * 8, 128), 1) == y)
    gram[:, 0:128] = jnp.where(mine, energy, gram[:, 0:128])

    piece = y * 2 + core

    def piece_copy(k):
        to = lax.rem(piece + k, 8)
        return pltpu.make_async_remote_copy(
            src_ref=gram.at[pl.ds(pl.multiple_of(to * 64, 64), 64)], dst_ref=d1.at[piece],
            send_sem=d1_ss, recv_sem=d1_rs,
            device_id={"vir": chip * 2 + lax.rem(to, 2), "trip": to // 2}, device_id_type=MESH,
        )

    for k in range(1, 8):
        piece_copy(k).start()
    pltpu.make_async_copy(
        gram.at[pl.ds(pl.multiple_of(piece * 64, 64), 64)], d1.at[piece], d1_rs
    ).start()

    send_b(yb_send, yb_recv, 3, yb_rs.at[grp], 0, 2)

    pltpu.make_async_copy(d1, d1, d1_rs).wait()
    d2s[...] = jnp.sum(d1[...], axis=0)

    def owner_send(o, c):
        to = piece * 8 + o
        src = d2s.at[pl.ds(pl.multiple_of(o * 8, 8), 8)]

        @pl.when(to != v)
        def _():
            pltpu.make_async_remote_copy(
                src_ref=src, dst_ref=d2.at[chip], send_sem=d2_ss, recv_sem=d2_rs,
                device_id={"vir": to, "trip": y}, device_id_type=MESH,
            ).start()

        @pl.when(to == v)
        def _():
            pltpu.make_async_copy(src, d2.at[chip], d2_rs).start()

        return c

    lax.fori_loop(0, 8, owner_send, 0)

    send_b(yb_send, yb_recv, 3, yb_rs.at[grp], 2, GROUPS)

    all_of(ya_send, ya_recv, 2).wait_recv()

    def take_a(g, c):
        spread_a(ya_recv[slots_of(g), 0:48], ya_recv[slots_of(g), 48:96], tmp)
        o = nn(up[...], tmp[...]).reshape(L, GR, 256)
        gk[:, rows_of(g), 0:256] = o.astype(BF)
        return c

    lax.fori_loop(0, GROUPS, take_a, 0)

    def out_first(c, carry):
        x = gk[c, :, 0:256]
        r = tn(x, tij[...])
        top = r.astype(BF)
        low = (r - top.astype(F32)).astype(BF)
        cs[c] = nt(x, tijp[:, 0:256]) + (nn(pmt[:, 0:256], top) + nn(pmt[:, 0:256], low))
        return carry

    lax.fori_loop(0, L, out_first, 0)

    is_owner = y == grp

    def fin_copy(ty):
        return pltpu.make_async_remote_copy(
            src_ref=dfin, dst_ref=dfin, send_sem=d3_ss, recv_sem=d3_rs,
            device_id={"vir": v, "trip": ty}, device_id_type=MESH,
        )

    def take_b(s, c):
        g = group_at(s)
        pltpu.make_async_copy(yb_recv.at[slots_of(g)], yb_recv.at[slots_of(g)], yb_rs.at[g]).wait()
        last = spread_b(yb_recv[slots_of(g), 0:48], yb_recv[slots_of(g), 48:80], tmp)
        o = nn(up[...], tmp[...]).astype(BF)[:, 0:192]
        t = tij[rows_of(g), :]
        m = nt(o, tijp[:, 256:V]).reshape(L, GR, V)
        cs[:, rows_of(g), :] = cs[:, rows_of(g), :] + m
        for i in range(L):
            w[i, 0:192, 0:V] = w[i, 0:192, 0:V] + tn(o[GR * i : GR * (i + 1)], t)
        z = nn(ulast[...], last).astype(BF)
        cs[L - 1, rows_of(g), :] = cs[L - 1, rows_of(g), :] + nt(z, tijp[:, 0:256])
        w[0, 192:V, 0:V] = w[0, 192:V, 0:V] + tn(z, t)
        pltpu.make_async_copy(
            cs.at[:, rows_of(g)], cs_hbm.at[:, rows_of(g)], ld.at[2]
        ).start()
        return c

    w[:, 0:192, :] = jnp.zeros((L, 192, 512), F32)
    w[0, 192:V, :] = jnp.zeros((256, 512), F32)
    lax.fori_loop(0, 1, take_b, 0)

    @pl.when(is_owner)
    def _():
        pltpu.make_async_copy(d2, d2, d2_rs).wait()
        dfin[...] = jnp.sum(d2[...], axis=0)
        for dy in (1, 2, 3):
            fin_copy(lax.rem(y + dy, 4)).start()

    lax.fori_loop(1, GROUPS, take_b, 0)
    gi[:, 0:192, :] = w[:, 0:192, 0:V].astype(BF)
    gk[0, 0:256, :] = w[0, 192:V, 0:V].astype(BF)
    out_r = pltpu.make_async_copy(gi.at[:, pl.ds(0, 192)], r_hbm, ld.at[3])
    out_l = pltpu.make_async_copy(gk.at[0, pl.ds(0, 256)], rl_hbm, ld.at[4])
    out_r.start()
    out_l.start()

    @pl.when(jnp.logical_not(is_owner))
    def _():
        fin_copy(y).wait_recv()

    small[...] = dfin[...] * (1.0 / (V * V))
    sel = iota((1, 128), 1) == y
    es = jnp.sum(jnp.where(sel, dfin[7:8, 0:128], 0.0), axis=1, keepdims=True)
    small[7:8, 0:128] = jnp.broadcast_to(es * (1.0 / V**3), (1, 128))

    out_p.wait()
    pltpu.make_async_copy(cs, cs_hbm, ld.at[2]).wait()
    out_r.wait()
    out_l.wait()
    for h in range(2):
        part = g_send.at[0, pl.ds(0, N - 1)]
        pltpu.make_async_remote_copy(
            src_ref=part, dst_ref=part, send_sem=g_ss.at[h], recv_sem=y_l.at[0],
            device_id={"vir": v, "trip": up_y}, device_id_type=MESH,
        ).wait_send()
        for s in range(GROUPS):
            part = g_send.at[0, pl.ds(0, 2 * GD)]
            pltpu.make_async_remote_copy(
                src_ref=part, dst_ref=part, send_sem=y_ss.at[GROUPS * h + s], recv_sem=y_l.at[0],
                device_id={"vir": v, "trip": up_y}, device_id_type=MESH,
            ).wait_send()
            y_copy(h, y, s, up_y, y_l.at[0], y_fs).wait_send()
    for n, buf in enumerate((sa_send, sb_send, ya_send, yb_send)):
        part = buf.at[pl.ds(0, N - 1)]
        all_of(part, part, n).wait_send()
    part = d1.at[pl.ds(0, 7)]
    pltpu.make_async_remote_copy(
        src_ref=part, dst_ref=part, send_sem=d1_ss, recv_sem=d1_ss,
        device_id={"vir": v, "trip": up_y}, device_id_type=MESH,
    ).wait_send()

    def drain_owner(count):
        q = d2.at[pl.ds(0, count)]
        pltpu.make_async_remote_copy(
            src_ref=q, dst_ref=q, send_sem=d2_ss, recv_sem=d2_ss,
            device_id={"vir": v, "trip": up_y}, device_id_type=MESH,
        ).wait_send()

    own_piece = (v // 8) == piece

    @pl.when(own_piece)
    def _():
        drain_owner(7)

    @pl.when(jnp.logical_not(own_piece))
    def _():
        drain_owner(8)

    @pl.when(is_owner)
    def _():
        for dy in (1, 2, 3):
            fin_copy(lax.rem(y + dy, 4)).wait_send()


def finish(small, cs, r, rl, pmt, energy, density, vvvo):
    c = pl.program_id(0)
    acc = cs[0] + nn(pmt[:, 256:V], r[0])

    @pl.when(c < L - 1)
    def _():
        vvvo[0, 0] = acc.astype(BF)

    @pl.when(c == L - 1)
    def _():
        vvvo[0, 0] = (acc + nn(pmt[:, 0:256], rl[...])).astype(BF)
        density[...] = small[0:7, 0:V]
        energy[0] = jnp.sum(jnp.where(iota((1, 128), 1) == 0, small[7:8, 0:128], 0.0))


def body(triplets, pair_integrals, k_integrals, pair_amplitudes, k_amplitudes, occ_energy, vir_energy):
    vm = pl.BlockSpec(memory_space=pltpu.VMEM)
    sm = pl.BlockSpec(memory_space=pltpu.SMEM)
    hbm = pl.BlockSpec(memory_space=pl.ANY)
    slab = pltpu.VMEM((L, V, V), BF)
    dma = pltpu.SemaphoreType.DMA
    small, cs, r, rl, pmt = pl.pallas_call(
        kernel,
        out_shape=(
            jax.ShapeDtypeStruct((8, 512), F32),
            jax.ShapeDtypeStruct((L, V, V), F32),
            jax.ShapeDtypeStruct((L, 192, V), BF),
            jax.ShapeDtypeStruct((256, V), BF),
            jax.ShapeDtypeStruct((V, V), BF),
        ),
        in_specs=[sm, sm, sm, vm] + [hbm] * 7 + [vm] * 4,
        out_specs=(vm, hbm, hbm, hbm, hbm),
        scratch_shapes=[
            slab, slab, slab,
            pltpu.VMEM((V, V), BF),
            pltpu.VMEM((1, 2, V, V), BF),
            pltpu.VMEM((GD * SLOT, L * GR), BF),
            pltpu.VMEM((L * GR, GD * SLOT), BF),
            pltpu.VMEM((N * 8, V), BF),
            pltpu.VMEM((L, V, V), F32),
            pltpu.VMEM((L, V, 512), F32),
            pltpu.VMEM((L, V, 512), BF),
        ]
        + [pltpu.VMEM((V, V), BF)] * 6
        + [
            pltpu.VMEM((8, 512), F32),
            pltpu.VMEM((GD * SLOT, 256), BF),
            pltpu.VMEM((GD * 32, 512), BF),
            pltpu.VMEM((2, N, 32, 128), BF),
            pltpu.VMEM((2, 4, N, 32, 128), BF),
            pltpu.VMEM((N, ROWS_A, 128), BF),
            pltpu.VMEM((N, ROWS_A, 128), BF),
            pltpu.VMEM((N, ROWS_B, 128), BF),
            pltpu.VMEM((N, ROWS_B, 128), BF),
            pltpu.VMEM((N, ROWS_A, 128), BF),
            pltpu.VMEM((N, ROWS_A, 128), BF),
            pltpu.VMEM((N, ROWS_B, 128), BF),
            pltpu.VMEM((N, ROWS_B, 128), BF),
            pltpu.VMEM((N * 8, 512), F32),
            pltpu.VMEM((8, 64, 512), F32),
            pltpu.VMEM((32, 8, 512), F32),
            pltpu.VMEM((64, 512), F32),
            pltpu.VMEM((8, 512), F32),
            dma((8,)), dma((2,)), dma((8,)), dma((8,)), dma((8,)), dma((8,)), dma((8,)), dma((8,)),
            dma((4,)), dma((4,)), dma((4,)), dma, dma, dma, dma, dma, dma,
        ],
        compiler_params=pltpu.CompilerParams(
            collective_id=0, has_side_effects=True, vmem_limit_bytes=60 * 1024 * 1024
        ),
        name="triples",
    )(
        triplets, occ_energy, vir_energy, vir_energy.reshape(1, V), pair_integrals, k_integrals,
        pair_amplitudes, k_amplitudes,
        jnp.asarray(pack_matrix(), BF), jnp.asarray(unpack_matrix(), BF), jnp.asarray(row_matrix(), BF),
        jnp.asarray(pack_last(), BF), jnp.asarray(unpack_last(), BF),
        jnp.asarray(turn_pack_matrix(), BF), jnp.asarray(turn_unpack_matrix(), BF),
    )
    whole = lambda shape: pl.BlockSpec(shape, lambda c: (0,) * len(shape))
    return pl.pallas_call(
        finish,
        grid=(L,),
        out_shape=(
            jax.ShapeDtypeStruct((1,), F32),
            jax.ShapeDtypeStruct((L, V), F32),
            jax.ShapeDtypeStruct((1, L, V, V), BF),
        ),
        in_specs=[
            whole((8, 512)),
            pl.BlockSpec((1, V, V), lambda c: (c, 0, 0)),
            pl.BlockSpec((1, 192, V), lambda c: (c, 0, 0)),
            whole((256, V)),
            whole((V, V)),
        ],
        out_specs=(
            pl.BlockSpec(memory_space=pltpu.SMEM),
            whole((L, V)),
            pl.BlockSpec((1, 1, V, V), lambda c: (0, c, 0, 0)),
        ),
        compiler_params=pltpu.CompilerParams(vmem_limit_bytes=60 * 1024 * 1024),
        name="finish",
    )(small, cs, r, rl, pmt)


def solution(mesh):
    return jax.shard_map(
        body,
        mesh=mesh,
        in_specs=(
            P("trip", None),
            P(None, "vir", None, None),
            P("trip", "vir", None, None),
            P(),
            P("trip", None, None, None),
            P(),
            P(),
        ),
        out_specs=(P("trip"), P("vir", None), P("trip", "vir", None, None)),
        check_vma=False,
    )
```
